1024 devices in a mesh: lon: 128 (over z, y), lat: 8 (over x, core).
Axes of the slice: x: 4, y: 8, z: 16, core: 2. Of those that a mesh axis runs over, the one named last changes fastest.
Arguments:
- features: bfloat16 [32, 2048, 1024], P(None, 'lon', 'lat'), may hold values from -6 to 6
- velocity: float32 [8, 2048, 1024], P(None, 'lon', 'lat'), may hold values from -6 to 6
- velocity_cot: float32 [8, 2048, 1024], P(None, 'lon', 'lat'), may hold values from -6 to 6
- surface_cot: float32 [2048, 1024], P('lon', 'lat'), may hold values from -6 to 6
- damping: float32 [2048, 1024], P('lon', 'lat'), may hold values from 0.05 to 1
- wet_mask: int32 [2048, 1024], P('lon', 'lat'), may hold values 0 or 1
- aggregate_map: int32 [2048, 1024], P('lon', 'lat'), may hold values from 0 to 7
- coarse_inverse: float32 [8192, 8192], P(('lon', 'lat')), as said below
- conv_weight: bfloat16 [64, 288], replicated, may hold values from -0.375 to 0.375
- conv_bias: float32 [64], replicated, may hold values from -3 to 3
- out_weight: float32 [64], replicated, may hold values from -0.75 to 0.75
- level_weight: float32 [8], replicated, may hold values from 0.5 to 1.5
Outputs:
- grad_velocity: float32 [8, 2048, 1024], P(None, 'lon', 'lat')
- grad_conv_weight: float32 [64, 288], replicated
- grad_conv_bias: float32 [64], replicated
- grad_out_weight: float32 [64], replicated
The draws below stay inside these ranges and needn't reach their ends.
Inputs may be any that keep to these rules, and one draw needn't show every extreme that they name: `coarse_inverse`: symmetric and positive definite.
All inputs are finite; a program needn't handle non-finite values. No bound on the sum of `wet_mask` on one device may be relied on, other than what follows from the above.
Results may differ from the reference program's by a relative error of at most 0.013.
Values sent between devices are 32-bit elements; how exact they have to be, the bound alone decides.
No kernel may reach another device: no remote copies, remote signals or barrier semaphores. Data moves between devices by JAX's collectives and lax.ppermute only.
A program may use at most 32 MiB of HBM per device.

```python
import math
import jax
import jax.numpy as jnp
from jax import lax

CLON = 16
CLAT = 128
LEV = 8
CIN = 32
HID = 64
ITERS = 2
AGG = 8
NLON = 2048
NLAT = 1024
NCO = 8192
CNT = 256
N_LON = 128
N_LAT = 8


def draw_coarse_inverse(key, part):
    key = jax.random.fold_in(key, 7)
    first, second, third = jax.random.split(key, 3)
    noise = jnp.clip(jax.random.normal(first, (NCO, NCO), jnp.float32), -4.0, 4.0)
    noise = (noise + noise.T) * (0.25 / math.sqrt(2.0 * NCO))
    owners = NCO // AGG
    tile_of = jnp.arange(NCO, dtype=jnp.int32) // AGG
    partner = (tile_of + owners // 2) % owners
    paired = (partner[:, None] == tile_of[None, :]).astype(jnp.float32)
    coupling = jax.random.uniform(third, (NCO, NCO), jnp.float32, -0.4 / AGG, 0.4 / AGG) * paired
    coupling = 0.5 * (coupling + coupling.T)
    diagonal = jax.random.uniform(second, (NCO,), jnp.float32, 1.0, 2.0)
    return noise + coupling + jnp.diag(diagonal)


def touch_ends(values, own_key, smallest, largest):
    extent = values.shape
    index_at = [jax.random.randint(jax.random.fold_in(own_key, axis), (), 0, extent[axis]) for axis in range(len(extent))]
    values = values.at[tuple(index_at)].set(smallest)
    longest = extent.index(max(extent))
    index_at[longest] = (index_at[longest] + 1) % extent[longest]
    return values.at[tuple(index_at)].set(largest)


def steps_of(rng, extent, cuts, smallest, top_value):
    def one(position, parts):
        steps = jax.random.uniform(jax.random.fold_in(jax.random.fold_in(rng, 6), position), (parts,), jnp.float32, smallest / len(cuts), top_value / len(cuts))
        return jnp.repeat(jnp.exp(steps), extent[position] // parts).reshape((-1,) + (1,) * (len(extent) - position - 1))

    loudness = one(*cuts[0])
    for cut in cuts[1:]:
        loudness = loudness * one(*cut)
    return loudness


def normal_values(key, dims, scale, reach, cuts=(), held_as=jnp.bfloat16):
    values = jax.random.normal(key, dims, jnp.float32) * scale
    if len(cuts) > 0:
        values = steps_of(key, dims, cuts, -0.22, 0.18) * values
    return jnp.clip(values, min=-reach, max=reach).astype(held_as)


def setup_inputs(seed: int = 0) -> dict:
    seeds = jax.random.split(jax.random.key(seed), 13)
    features = normal_values(seeds[0], (CIN, NLON, NLAT), 1.0, 6.0, ((1, 128), (2, 8)))
    velocity = normal_values(seeds[1], (LEV, NLON, NLAT), 1.0, 6.0, ((1, 128), (2, 8)), jnp.float32)
    velocity_cot = normal_values(seeds[2], (LEV, NLON, NLAT), 1.0, 6.0, ((1, 128), (2, 8)), jnp.float32)
    surface_cot = normal_values(seeds[3], (NLON, NLAT), 1.0, 6.0, ((0, 128), (1, 8)), jnp.float32)
    damping = jnp.clip(jnp.exp(math.log(1.0) - 2.9957323 * jax.random.uniform(seeds[4], (NLON, NLAT), jnp.float32) ** steps_of(seeds[4], (NLON, NLAT), ((0, 128), (1, 8)), -0.2, 0.2)), 0.05, 1.0)
    wet_mask = touch_ends((jax.random.randint(seeds[5], (NLON, NLAT), 0, 5) < 4).astype(jnp.int32), jax.random.fold_in(seeds[5], 1), 0, 1)
    aggregate_map = touch_ends(jax.random.randint(seeds[6], (NLON, NLAT), 0, AGG), jax.random.fold_in(seeds[6], 1), 0, AGG - 1).astype(jnp.int32)
    coarse_inverse = draw_coarse_inverse(jax.random.fold_in(seeds[12], 71), 0)
    conv_weight = normal_values(seeds[8], (HID, 9 * CIN), (9 * CIN) ** -0.5, 0.375)
    conv_bias = normal_values(seeds[9], (HID,), 0.5, 3.0, (), jnp.float32)
    out_weight = normal_values(seeds[10], (HID,), HID ** -0.5, 0.75, (), jnp.float32)
    level_weight = jnp.clip(jax.random.uniform(seeds[11], (LEV,), jnp.float32, 0.5, 1.5), 0.5, 1.5)
    return dict(features=features, velocity=velocity, velocity_cot=velocity_cot, surface_cot=surface_cot, damping=damping, wet_mask=wet_mask, aggregate_map=aggregate_map, coarse_inverse=coarse_inverse, conv_weight=conv_weight, conv_bias=conv_bias, out_weight=out_weight, level_weight=level_weight)


time_step = 0.1

def widen(field):
    rows = jnp.concatenate([field[..., -1:, :], field, field[..., :1, :]], axis=-2)
    return jnp.pad(rows, [(0, 0)] * (field.ndim - 1) + [(1, 1)])

def neighbours(padded):
    return (padded[..., 2:, 1:-1], padded[..., :-2, 1:-1], padded[..., 1:-1, 2:], padded[..., 1:-1, :-2])

def side_total(padded):
    north, south, east, west = neighbours(padded)
    return north + south + east + west

def patches_of(block):
    rows = block.shape[-2] - 2
    width = block.shape[-1] - 2
    taps = [block[:, first:first + rows, second:second + width] for first in range(3) for second in range(3)]
    return jnp.concatenate(taps, axis=0).reshape(-1, rows * width)

def reference(features, velocity, velocity_cot, surface_cot, damping, wet_mask, aggregate_map, coarse_inverse, conv_weight, conv_bias, out_weight, level_weight):
    wet = wet_mask.astype(jnp.float32)
    diagonal = 4.0 + damping
    padded = widen(features)

    def hidden_of(index):
        start = (index * CLON).astype(jnp.int32)
        block = lax.dynamic_slice_in_dim(padded, start, CLON + 2, 1)
        columns = patches_of(block)
        preact = jnp.dot(conv_weight, columns, preferred_element_type=jnp.float32) + conv_bias[:, None]
        return (columns, jnp.tanh(preact))

    def forward_block(index):
        columns, hidden = hidden_of(index)
        return lax.optimization_barrier(jnp.sum(out_weight[:, None] * hidden, axis=0)).reshape(CLON, NLAT)
    logits = lax.map(forward_block, jnp.arange(N_LON, dtype=jnp.int32)).reshape(NLON, NLAT)
    viscosity = jax.nn.softplus(logits)
    lon_block = (jnp.arange(NLON, dtype=jnp.int32) // CLON)[:, None]
    lat_block = (jnp.arange(NLAT, dtype=jnp.int32) // CLAT)[None, :]
    coarse_id = ((lon_block * N_LAT + lat_block) * AGG + aggregate_map).reshape(-1).astype(jnp.int32)

    def operate(field):
        return diagonal * field - wet * side_total(widen(wet * field))

    def precondition(residual):
        local = jax.ops.segment_sum(residual.reshape(-1), coarse_id, num_segments=NCO) / math.sqrt(CNT)
        fix = jnp.dot(coarse_inverse, local, precision=lax.Precision.HIGHEST)
        return residual / diagonal + fix[coarse_id].reshape(NLON, NLAT)
    solution = jnp.zeros((NLON, NLAT), jnp.float32)
    residual = surface_cot
    search = precondition(residual)
    energy = jnp.sum(residual * search)
    for step in range(ITERS):
        image = operate(search)
        step_size = energy / jnp.sum(search * image)
        solution = solution + step_size * search
        residual = residual - step_size * image
        if step + 1 < ITERS:
            smoothed = precondition(residual)
            energy_next = jnp.sum(residual * smoothed)
            search = smoothed + energy_next / energy * search
            energy = energy_next
    forcing = side_total(widen(wet * solution)) - 4.0 * wet * solution
    adjoint_vel = velocity_cot + level_weight[:, None, None] * forcing[None]
    visc_pad = widen(viscosity)
    vel_pad = widen(velocity)
    adj_pad = widen(adjoint_vel)
    spread = jnp.zeros_like(adjoint_vel)
    grad_visc = jnp.zeros_like(viscosity)
    for visc_side, vel_side, adj_side in zip(neighbours(visc_pad), neighbours(vel_pad), neighbours(adj_pad)):
        change = adj_side - adjoint_vel
        spread = spread + 0.5 * (viscosity + visc_side)[None] * change
        grad_visc = grad_visc + lax.optimization_barrier(jnp.sum((vel_side - velocity) * change, axis=0))
    grad_velocity = adjoint_vel + time_step * spread
    grad_visc = -0.5 * time_step * grad_visc
    grad_logit = grad_visc * jax.nn.sigmoid(logits) / math.sqrt(NLON * NLAT)

    def backward_block(carry, index):
        weight_grad, bias_grad, out_grad = carry
        columns, hidden = hidden_of(index)
        start = (index * CLON).astype(jnp.int32)
        local = lax.dynamic_slice_in_dim(grad_logit, start, CLON, 0).reshape(-1)
        out_grad = out_grad + lax.optimization_barrier(jnp.sum(hidden * local[None], axis=1))
        grad_pre = (local[None] * out_weight[:, None] * (1.0 - hidden * hidden)).astype(jnp.bfloat16)
        bias_grad = bias_grad + lax.optimization_barrier(jnp.sum(grad_pre.astype(jnp.float32), axis=1))
        weight_grad = weight_grad + jnp.dot(grad_pre, columns.T, preferred_element_type=jnp.float32)
        return ((weight_grad, bias_grad, out_grad), None)
    start_carry = (jnp.zeros((HID, 9 * CIN), jnp.float32), jnp.zeros((HID,), jnp.float32), jnp.zeros((HID,), jnp.float32))
    grads, unused = lax.scan(backward_block, start_carry, jnp.arange(N_LON, dtype=jnp.int32))
    return (grad_velocity, grads[0], grads[1], grads[2])
```

```python
import math

import jax
import jax.numpy as jnp
import numpy as np
from jax import lax
from jax.experimental import pallas as pl
from jax.experimental.pallas import tpu as pltpu
from jax.sharding import Mesh
from jax.sharding import PartitionSpec as P

CIN = 32
HID = 64
AGG = 8
CNT = 256
TAPS = 9 * CIN
time_step = 0.1

CLON = 16
CLAT = 128
HALO = 3
ROWS = 24
LANES = 256
LON = ("z", "y")
LAT = ("x", "c")
PLANE = ("y", "x")
COLUMN = ("z", "c")


def exchange(values, axes):
    return lax.all_to_all(values, axes, 0, 0, tiled=True)


def shifted(block, axes, periodic):
    count = lax.axis_size(axes)
    forward = [(i, i + 1) for i in range(count - 1)]
    if periodic:
        forward.append((count - 1, 0))
    return forward, [(target, source) for source, target in forward]


def ring_lanes(own, right, left):
    gap = LANES - CLAT - right.shape[-1] - left.shape[-1]
    return jnp.concatenate([own, right, jnp.zeros(own.shape[:-1] + (gap,), own.dtype), left], axis=-1)


def ring_rows(own, below, above):
    gap = ROWS - CLON - below.shape[-2] - above.shape[-2]
    shape = own.shape[:-2] + (gap, own.shape[-1])
    return jnp.concatenate([own, below, jnp.zeros(shape, own.dtype), above], axis=-2)


def roll(value, shift, axis):
    return pltpu.roll(value, shift % value.shape[axis], axis)


def sides(value):
    return (roll(value, -1, 0), roll(value, 1, 0), roll(value, -1, 1), roll(value, 1, 1))


def side_sum(value):
    a, b, c, d = sides(value)
    return (a + b) + (c + d)


def coarse_column(tiles, groups, vector):
    count = vector.shape[0]
    out = []
    for group in range(groups):
        acc = tiles[group * count] * vector[0:1]
        for k in range(1, count):
            acc = acc + tiles[group * count + k] * vector[k : k + 1]
        out.append(jnp.sum(acc, axis=1, keepdims=True))
    return out


def coarse_field(agg, above, middle, below):
    lane = lax.broadcasted_iota(jnp.int32, (1, CLAT), 1)
    row = lax.broadcasted_iota(jnp.int32, (ROWS - CLON, LANES), 0)

    def across(columns, k):
        left, own, right = (column[k : k + 1] for column in columns)
        side = jnp.where(lane < CLAT // 2, right, left)
        return jnp.concatenate([jnp.broadcast_to(own, (1, CLAT)), side], axis=1)

    field = jnp.zeros((ROWS, LANES), jnp.float32)
    for k in range(AGG):
        inner = jnp.broadcast_to(across(middle, k), (CLON, LANES))
        outer = jnp.where(row < (ROWS - CLON) // 2, across(below, k), across(above, k))
        field = jnp.where(agg == float(k), jnp.concatenate([inner, outer], axis=0), field)
    return field


def total(value):
    return jnp.sum(jnp.sum(value, axis=0, keepdims=True), axis=1, keepdims=True)


def restricted(value, agg, first):
    parts = [jnp.sum(jnp.where(agg == float(k), value, 0.0), axis=0, keepdims=True) for k in range(AGG)]
    sums = jnp.sum(jnp.concatenate(parts, axis=0), axis=1, keepdims=True) * (1.0 / math.sqrt(CNT))
    lane = lax.broadcasted_iota(jnp.int32, (AGG, 128), 1)
    row = lax.broadcasted_iota(jnp.int32, (AGG, 128), 0)
    return jnp.sum(jnp.where(lane == first + row, sums, 0.0), axis=0, keepdims=True)


def vector_of(ref, packed):
    count = ref.shape[0] // packed
    value = ref[pl.ds(0, count, stride=packed), :]
    for t in range(1, packed):
        value = value + ref[pl.ds(t, count, stride=packed), :]
    return value


def solve_first(packed, place, gathered, tiles_own, tiles_below, tiles_above, fields, w_ref, f_ref, z_ref, row_ref, sum_ref):
    vector = vector_of(gathered, packed)
    rhs, damp, wet, agg = (fields[k] for k in range(4))
    diagonal = 4.0 + damp
    middle = coarse_column(tiles_own, 3, vector)
    below = coarse_column(tiles_below, 3, vector)
    above = coarse_column(tiles_above, 3, vector)
    z = rhs / diagonal + coarse_field(agg, above, middle, below)
    spread = side_sum(wet * z)
    w = diagonal * z - wet * spread
    w_ref[...] = w
    f_ref[...] = spread - 4.0 * wet * z
    own = (slice(0, CLON), slice(0, CLAT))
    z_own, w_own = z[own], w[own]
    z_ref[...] = z_own
    row_ref[...] = restricted(w_own, agg[own], place[0])
    lane = lax.broadcasted_iota(jnp.int32, (1, 128), 1)
    sum_ref[...] = jnp.where(lane == 0, total(rhs[own] * z_own), 0.0) + jnp.where(lane == 1, total(z_own * w_own), 0.0)


def solve_second(
    packed, gathered, tiles_own, tiles_below, tiles_above, fields, w_ref, f_ref, visc_ref, valid_ref, weight_ref,
    slope_ref, first_ref, sum_in, grad_ref, spread_ref, sum_ref,
):
    vector = vector_of(gathered, packed)
    rhs, damp, wet, agg = (fields[k] for k in range(4))
    diagonal = 4.0 + damp
    w = w_ref[...]
    middle = coarse_column(tiles_own, 3, vector)
    below = coarse_column(tiles_below, 3, vector)
    above = coarse_column(tiles_above, 3, vector)
    y = w / diagonal + coarse_field(agg, above, middle, below)
    around = side_sum(wet * y)
    image = diagonal * y - wet * around
    own = (slice(0, CLON), slice(0, CLAT))
    y_own = y[own]
    lane = lax.broadcasted_iota(jnp.int32, (1, 128), 1)
    sums = sum_in[...]
    for at, value in ((2, rhs[own] * y_own), (3, w[own] * y_own), (4, y_own * image[own])):
        sums = sums + jnp.where(lane == at, total(value), 0.0)
    sum_ref[...] = sums
    visc = visc_ref[...]
    visc_own = visc[own]
    visc_sides = [0.5 * (visc_own + side[own]) for side in sides(visc)]
    valid = valid_ref[...]
    weight = weight_ref[...]
    grad_ref[0] = first_ref[...] * weight
    for at, force in ((0, f_ref[...] * valid), (1, (around - 4.0 * wet * y) * valid)):
        force_own = force[own]
        bend = jnp.zeros((CLON, CLAT), jnp.float32)
        slope = jnp.zeros((CLON, CLAT), jnp.float32)
        for n, side in enumerate(sides(force)):
            change = side[own] - force_own
            bend = bend + visc_sides[n] * change
            slope = slope + slope_ref[n] * change
        spread_ref[at] = force_own + time_step * bend
        grad_ref[at + 1] = slope * weight


def neighbours(padded):
    return (padded[..., 2:, 1:-1], padded[..., :-2, 1:-1], padded[..., 1:-1, 2:], padded[..., 1:-1, :-2])


def patches_of(block):
    rows = block.shape[-2] - 2
    width = block.shape[-1] - 2
    taps = [
        block[:, first : first + rows, second : second + width]
        for first in range(3)
        for second in range(3)
    ]
    return jnp.concatenate(taps, axis=0).reshape(-1, rows * width)


def tiles_of(rows):
    count, width = rows.shape
    return rows.reshape(count // 8, 8, width // 128, 128).transpose(0, 2, 1, 3).reshape(-1, 8, 128)


def rows_of(tiles, count):
    return tiles.reshape(count // 8, -1, 8, 128).transpose(0, 2, 1, 3).reshape(count, -1)


def kernel_call(body, shapes, *args, smem=0):
    specs = [pl.BlockSpec(memory_space=pltpu.SMEM)] * smem + [pl.BlockSpec(memory_space=pltpu.VMEM)] * (len(args) - smem)
    return pl.pallas_call(
        body,
        out_shape=[jax.ShapeDtypeStruct(shape, jnp.float32) for shape in shapes],
        in_specs=specs,
        out_specs=[pl.BlockSpec(memory_space=pltpu.VMEM)] * len(shapes),
        compiler_params=pltpu.CompilerParams(vmem_limit_bytes=24 * 1024 * 1024),
    )(*args)


def shards(
    features,
    velocity,
    velocity_cot,
    surface_cot,
    damping,
    wet_mask,
    aggregate_map,
    coarse_inverse,
    conv_weight,
    conv_bias,
    out_weight,
    level_weight,
):
    f32 = jnp.float32
    n_lon, n_lat = lax.axis_size(LON), lax.axis_size(LAT)
    lon, lat = lax.axis_index(LON), lax.axis_index(LAT)
    per = n_lat * AGG
    packed = 128 // per
    place = (lat * AGG + (lon % packed) * per).astype(jnp.int32)

    single = jnp.concatenate([features.astype(f32), velocity, velocity_cot], axis=0)
    several = jnp.stack([surface_cot, damping, wet_mask.astype(f32), aggregate_map.astype(f32)])
    n_single, n_several = single.shape[0], several.shape[0]
    coarse = tiles_of(coarse_inverse)

    def side_tiles(line, block):
        edge = jnp.concatenate([line, block.transpose(0, 2, 1).reshape(-1, CLON)], axis=0)
        edge = jnp.pad(edge, ((0, 64 - edge.shape[0]), (0, 0))).reshape(1, 8, 128)
        return jnp.concatenate([coarse, edge], axis=0)

    forward, backward = shifted(single, LAT, False)
    left = lax.ppermute(side_tiles(single[:, :, -1], several[:, :, -HALO:]), LAT, forward)
    right = lax.ppermute(side_tiles(single[:, :, 0], several[:, :, :HALO]), LAT, backward)

    local = restricted(surface_cot, aggregate_map.astype(f32), place)

    def across_lat(rows):
        return exchange(rows, LAT)

    row = jnp.sum(across_lat(jnp.broadcast_to(local[None], (n_lat, 1, 128))), axis=0)
    row, left, right = lax.optimization_barrier((row, left, right))

    def unpack(tiles):
        edge = tiles[-1].reshape(64, CLON)
        block = edge[n_single : n_single + n_several * HALO].reshape(n_several, HALO, CLON)
        return tiles[:-1], edge[:n_single], block.transpose(0, 2, 1)

    coarse_left, line_left, block_left = unpack(left)
    coarse_right, line_right, block_right = unpack(right)
    band = jnp.concatenate([coarse_left, coarse, coarse_right], axis=0)
    several = ring_lanes(several, block_right, block_left)

    def end_tiles(at, block):
        line = ring_lanes(single[:, at, :], line_right[:, at : at + 1], line_left[:, at : at + 1])
        edge = jnp.concatenate([line, block.reshape(-1, LANES)], axis=0)
        edge = jnp.pad(edge, ((0, 64 - edge.shape[0]), (0, 0)))
        return jnp.concatenate([band, tiles_of(edge)], axis=0)

    forward, backward = shifted(single, LON, True)
    above = lax.ppermute(end_tiles(CLON - 1, several[:, -HALO:]), LON, forward)
    below = lax.ppermute(end_tiles(0, several[:, :HALO]), LON, backward)
    gathered = exchange(jnp.broadcast_to(row[None], (n_lon, 1, 128)), LON).reshape(n_lon, 128)
    gathered, above, below = lax.optimization_barrier((gathered, above, below))

    count = band.shape[0]

    def unpack_rows(tiles):
        edge = rows_of(tiles[count:], 64)
        block = edge[n_single : n_single + n_several * HALO].reshape(n_several, HALO, LANES)
        return tiles[:count], edge[:n_single], block

    band_above, line_above, block_above = unpack_rows(above)
    band_below, line_below, block_below = unpack_rows(below)
    fields = ring_rows(several, block_below, block_above)

    def padded(first, last):
        def ends(line):
            line = line[first:last]
            return jnp.concatenate([line[:, -1:], line[:, : CLAT + 1]], axis=1)[:, None]

        middle = jnp.concatenate(
            [line_left[first:last, :, None], single[first:last], line_right[first:last, :, None]], axis=2
        )
        return jnp.concatenate([ends(line_above), middle, ends(line_below)], axis=1)

    levels = velocity.shape[0]
    feat_pad = padded(0, CIN).astype(jnp.bfloat16)
    vel_pad = padded(CIN, CIN + levels)
    cot_pad = padded(CIN + levels, CIN + 2 * levels)

    w, force, z, row, sums = kernel_call(
        lambda *refs: solve_first(packed, *refs),
        [(ROWS, LANES), (ROWS, LANES), (CLON, CLAT), (1, 128), (1, 128)],
        place[None],
        gathered,
        band,
        band_below,
        band_above,
        fields,
        smem=1,
    )

    columns = patches_of(feat_pad)
    hidden = jnp.tanh(jnp.dot(conv_weight, columns, preferred_element_type=f32) + conv_bias[:, None])
    logits = jnp.sum(out_weight[:, None] * hidden, axis=0).reshape(CLON, CLAT)
    viscosity = jax.nn.softplus(logits)

    to = jnp.arange(n_lat)[:, None]
    first_col = jnp.pad(viscosity[:, 0], (0, 128 - CLON))[None]
    last_col = jnp.pad(viscosity[:, -1], (0, 128 - CLON))[None]
    edge = jnp.where(to == lat + 1, last_col, 0.0) + jnp.where(to == lat - 1, first_col, 0.0)
    sent = jnp.stack([jnp.broadcast_to(row, (n_lat, 128)), edge], axis=1)
    got = across_lat(sent)
    row = jnp.sum(got[:, 0], axis=0)
    visc_left = jnp.sum(jnp.where(to == lat - 1, got[:, 1], 0.0), axis=0)[:CLON, None]
    visc_right = jnp.sum(jnp.where(to == lat + 1, got[:, 1], 0.0), axis=0)[:CLON, None]
    to = jnp.arange(n_lon)[:, None]
    after, before = to == (lon + 1) % n_lon, to == (lon + n_lon - 1) % n_lon
    edge = jnp.where(after, viscosity[-1:], 0.0) + jnp.where(before, viscosity[:1], 0.0)
    sent = jnp.stack([jnp.broadcast_to(row[None], (n_lon, 128)), edge], axis=1)
    got = exchange(sent, LON)
    gathered = got[:, 0]
    visc_above = jnp.sum(jnp.where(before, got[:, 1], 0.0), axis=0)[None]
    visc_below = jnp.sum(jnp.where(after, got[:, 1], 0.0), axis=0)[None]

    def rim(line):
        return jnp.pad(line, ((0, 0), (0, LANES - CLAT)))

    visc = ring_rows(ring_lanes(viscosity, visc_right, visc_left), rim(visc_below), rim(visc_above))
    visc_pad = jnp.concatenate([visc[-1:], visc[: CLON + 1]], axis=0)
    visc_pad = jnp.concatenate([visc_pad[:, -1:], visc_pad[:, : CLAT + 1]], axis=1)

    lane = jnp.arange(LANES)[None]
    valid = jnp.where(lane < CLAT, 1.0, jnp.where(lane < CLAT + LANES // 4, lat < n_lat - 1, lat > 0).astype(f32))

    level = level_weight[:, None, None]
    base = jnp.zeros_like(velocity_cot)
    first = jnp.zeros_like(viscosity)
    slopes = []
    for visc_side, vel_side, cot_side in zip(neighbours(visc_pad), neighbours(vel_pad), neighbours(cot_pad)):
        change = cot_side - velocity_cot
        slope = vel_side - velocity
        base = base + 0.5 * (viscosity + visc_side)[None] * change
        first = first + jnp.sum(slope * change, axis=0)
        slopes.append(jnp.sum(level * slope, axis=0))
    base = velocity_cot + time_step * base
    cells_all = CLON * CLAT * n_lon * n_lat
    weight = jax.nn.sigmoid(logits) * (-0.5 * time_step / math.sqrt(cells_all))

    grads, spreads, sums = kernel_call(
        lambda *refs: solve_second(packed, *refs),
        [(3, CLON, CLAT), (2, CLON, CLAT), (1, 128)],
        gathered,
        band,
        band_below,
        band_above,
        fields,
        w,
        force,
        visc,
        valid,
        weight,
        jnp.stack(slopes),
        first,
        sums,
    )

    lines = grads.reshape(3, 1, CLON * CLAT)
    out_grad = jnp.sum(hidden[None] * lines, axis=2)
    pre = lines * (out_weight[:, None] * (1.0 - hidden * hidden))[None]
    bias_grad = jnp.sum(pre, axis=2)
    rounded = lax.reduce_precision(pre, 8, 7)
    high = rounded.astype(jnp.bfloat16)
    low = (pre - rounded).astype(jnp.bfloat16)

    def against(part):
        return lax.dot_general(
            part.reshape(3 * HID, -1), columns, (((1,), (1,)), ((), ())), preferred_element_type=f32
        )

    weight_grad = (against(high) + against(low)).reshape(3, HID, TAPS)
    table = jnp.concatenate([weight_grad, bias_grad[..., None], out_grad[..., None]], axis=2)
    width = table.shape[2]

    n_plane, n_column = lax.axis_size(PLANE), lax.axis_size(COLUMN)
    each = HID // n_plane
    sent = table.reshape(3, n_plane, each, width).transpose(1, 0, 2, 3).reshape(n_plane, 3 * each, width)
    sent = jnp.pad(sent, ((0, 0), (0, 0), (0, 384 - width)))
    extra = jnp.broadcast_to(jnp.pad(sums, ((0, 0), (0, 256)))[None], (n_plane, 1, 384))
    sent = jnp.concatenate([sent, extra], axis=1)
    sent = jnp.pad(sent, ((0, 0), (0, -sent.shape[1] % 8), (0, 0)))
    part = jnp.sum(exchange(sent, PLANE), axis=0)
    whole = jnp.sum(exchange(jnp.broadcast_to(part[None], (n_column,) + part.shape), COLUMN), axis=0)

    e0, d0, cross, ww, g = (whole[3 * each, k] for k in range(5))
    step0 = e0 / d0
    e1 = e0 - step0 * d0 - step0 * cross + step0 * step0 * ww
    beta = e1 / e0
    lead = 1.0 + beta
    pw = lead * lead * d0 - 2.0 * lead * step0 * ww + step0 * step0 * g
    step1 = e1 / pw
    on_z = step0 + step1 * lead
    on_y = -step1 * step0

    mine = whole[:each] + on_z * whole[each : 2 * each] + on_y * whole[2 * each : 3 * each]
    final = exchange(jnp.broadcast_to(mine[None], (n_plane,) + mine.shape), PLANE).reshape(HID, 384)
    grad_velocity = base + level * (on_z * spreads[0] + on_y * spreads[1])[None]
    return (grad_velocity, final[:, :TAPS], final[:, TAPS], final[:, TAPS + 1])


def solution(mesh):
    n_lon, n_lat = mesh.shape["lon"], mesh.shape["lat"]
    y = min(8, n_lon // 2)
    shape = (n_lon // y, y, n_lat // 2, 2)
    grid = Mesh(np.asarray(mesh.devices).reshape(shape), LON + LAT)
    tile = P(None, LON, LAT)
    flat = P(LON, LAT)
    in_specs = (tile, tile, tile, flat, flat, flat, flat, P(LON + LAT, None), P(), P(), P(), P())
    out_specs = (tile, P(), P(), P())
    return jax.shard_map(shards, mesh=grid, in_specs=in_specs, out_specs=out_specs, check_vma=False)
```

```python
import math

import jax
import jax.numpy as jnp
import numpy as np
from jax import lax
from jax.experimental import pallas as pl
from jax.experimental.pallas import tpu as pltpu
from jax.sharding import Mesh
from jax.sharding import PartitionSpec as P

CIN = 32
HID = 64
AGG = 8
CNT = 256
TAPS = 9 * CIN
time_step = 0.1

CLON = 16
CLAT = 128
HALO = 3
ROWS = 24
LANES = 256
LON = ("z", "y")
LAT = ("x", "c")
LAYER = ("y", "x", "c")
DEPTH = ("z",)
SPARE = 34


def exchange(values, axes):
    return lax.all_to_all(values, axes, 0, 0, tiled=True)


def shifted(block, axes, periodic):
    count = lax.axis_size(axes)
    forward = [(i, i + 1) for i in range(count - 1)]
    if periodic:
        forward.append((count - 1, 0))
    return forward, [(target, source) for source, target in forward]


def ring_lanes(own, right, left):
    gap = LANES - CLAT - right.shape[-1] - left.shape[-1]
    return jnp.concatenate([own, right, jnp.zeros(own.shape[:-1] + (gap,), own.dtype), left], axis=-1)


def ring_rows(own, below, above):
    gap = ROWS - CLON - below.shape[-2] - above.shape[-2]
    shape = own.shape[:-2] + (gap, own.shape[-1])
    return jnp.concatenate([own, below, jnp.zeros(shape, own.dtype), above], axis=-2)


def roll(value, shift, axis):
    return pltpu.roll(value, shift % value.shape[axis], axis)


def sides(value):
    return (roll(value, -1, 0), roll(value, 1, 0), roll(value, -1, 1), roll(value, 1, 1))


def side_sum(value):
    a, b, c, d = sides(value)
    return (a + b) + (c + d)


def coarse_column(tiles, groups, vector):
    count = vector.shape[0]
    out = []
    for group in range(groups):
        acc = tiles[group * count] * vector[0:1]
        for k in range(1, count):
            acc = acc + tiles[group * count + k] * vector[k : k + 1]
        out.append(jnp.sum(acc, axis=1, keepdims=True))
    return out


def coarse_field(agg, above, middle, below):
    lane = lax.broadcasted_iota(jnp.int32, (1, CLAT), 1)
    row = lax.broadcasted_iota(jnp.int32, (ROWS - CLON, LANES), 0)

    def across(columns, k):
        left, own, right = (column[k : k + 1] for column in columns)
        side = jnp.where(lane < CLAT // 2, right, left)
        return jnp.concatenate([jnp.broadcast_to(own, (1, CLAT)), side], axis=1)

    field = jnp.zeros((ROWS, LANES), jnp.float32)
    for k in range(AGG):
        inner = jnp.broadcast_to(across(middle, k), (CLON, LANES))
        outer = jnp.where(row < (ROWS - CLON) // 2, across(below, k), across(above, k))
        field = jnp.where(agg == float(k), jnp.concatenate([inner, outer], axis=0), field)
    return field


def total(value):
    return jnp.sum(jnp.sum(value, axis=0, keepdims=True), axis=1, keepdims=True)


def restricted(value, agg, first):
    parts = [jnp.sum(jnp.where(agg == float(k), value, 0.0), axis=0, keepdims=True) for k in range(AGG)]
    sums = jnp.sum(jnp.concatenate(parts, axis=0), axis=1, keepdims=True) * (1.0 / math.sqrt(CNT))
    lane = lax.broadcasted_iota(jnp.int32, (AGG, 128), 1)
    row = lax.broadcasted_iota(jnp.int32, (AGG, 128), 0)
    return jnp.sum(jnp.where(lane == first + row, sums, 0.0), axis=0, keepdims=True)


def solve_first(place, gathered, tiles_own, tiles_below, tiles_above, fields, w_ref, f_ref, z_ref, row_ref, sum_ref):
    vector = gathered[...]
    rhs, damp, wet, agg = (fields[k] for k in range(4))
    diagonal = 4.0 + damp
    middle = coarse_column(tiles_own, 3, vector)
    below = coarse_column(tiles_below, 3, vector)
    above = coarse_column(tiles_above, 3, vector)
    z = rhs / diagonal + coarse_field(agg, above, middle, below)
    spread = side_sum(wet * z)
    w = diagonal * z - wet * spread
    w_ref[...] = w
    f_ref[...] = spread - 4.0 * wet * z
    own = (slice(0, CLON), slice(0, CLAT))
    z_own, w_own = z[own], w[own]
    z_ref[...] = z_own
    row_ref[...] = restricted(w_own, agg[own], place[0])
    lane = lax.broadcasted_iota(jnp.int32, (1, 128), 1)
    sum_ref[...] = jnp.where(lane == 0, total(rhs[own] * z_own), 0.0) + jnp.where(lane == 1, total(z_own * w_own), 0.0)


def solve_second(
    gathered, tiles_own, tiles_below, tiles_above, fields, w_ref, f_ref, visc_ref, valid_ref, weight_ref,
    slope_ref, first_ref, sum_in, grad_ref, spread_ref, sum_ref,
):
    vector = gathered[...]
    rhs, damp, wet, agg = (fields[k] for k in range(4))
    diagonal = 4.0 + damp
    w = w_ref[...]
    middle = coarse_column(tiles_own, 3, vector)
    below = coarse_column(tiles_below, 3, vector)
    above = coarse_column(tiles_above, 3, vector)
    y = w / diagonal + coarse_field(agg, above, middle, below)
    around = side_sum(wet * y)
    image = diagonal * y - wet * around
    own = (slice(0, CLON), slice(0, CLAT))
    y_own = y[own]
    lane = lax.broadcasted_iota(jnp.int32, (1, 128), 1)
    sums = sum_in[...]
    for at, value in ((2, rhs[own] * y_own), (3, w[own] * y_own), (4, y_own * image[own])):
        sums = sums + jnp.where(lane == at, total(value), 0.0)
    sum_ref[...] = sums
    visc = visc_ref[...]
    visc_own = visc[own]
    visc_sides = [0.5 * (visc_own + side[own]) for side in sides(visc)]
    valid = valid_ref[...]
    weight = weight_ref[...]
    grad_ref[0] = first_ref[...] * weight
    for at, force in ((0, f_ref[...] * valid), (1, (around - 4.0 * wet * y) * valid)):
        force_own = force[own]
        bend = jnp.zeros((CLON, CLAT), jnp.float32)
        slope = jnp.zeros((CLON, CLAT), jnp.float32)
        for n, side in enumerate(sides(force)):
            change = side[own] - force_own
            bend = bend + visc_sides[n] * change
            slope = slope + slope_ref[n] * change
        spread_ref[at] = force_own + time_step * bend
        grad_ref[at + 1] = slope * weight


def finish(parts, spreads, mine_ref, spread_ref):
    row = jnp.sum(parts[...], axis=0)
    main, tail = 2 * 128, 6 * 128

    def scalar(k):
        at = tail + 3 * SPARE + k
        return row[:1, at : at + 1]

    e0, d0, cross, ww, g = (scalar(k) for k in range(5))
    step0 = e0 / d0
    e1 = e0 - step0 * d0 - step0 * cross + step0 * step0 * ww
    beta = e1 / e0
    lead = 1.0 + beta
    pw = lead * lead * d0 - 2.0 * lead * step0 * ww + step0 * step0 * g
    step1 = e1 / pw
    on_z = step0 + step1 * lead
    on_y = -step1 * step0
    front = row[:, :main] + on_z * row[:, main : 2 * main] + on_y * row[:, 2 * main : 3 * main]
    last = row[:, tail:]
    back = last + on_z * roll(last, -SPARE, 1) + on_y * roll(last, -2 * SPARE, 1)
    mine_ref[...] = jnp.concatenate([front, back], axis=1)
    spread_ref[...] = on_z * spreads[0] + on_y * spreads[1]


def neighbours(padded):
    return (padded[..., 2:, 1:-1], padded[..., :-2, 1:-1], padded[..., 1:-1, 2:], padded[..., 1:-1, :-2])


def patches_of(block):
    rows = block.shape[-2] - 2
    width = block.shape[-1] - 2
    taps = [
        block[:, first : first + rows, second : second + width]
        for first in range(3)
        for second in range(3)
    ]
    return jnp.concatenate(taps, axis=0).reshape(-1, rows * width)


def tiles_of(rows):
    count, width = rows.shape
    return rows.reshape(count // 8, 8, width // 128, 128).transpose(0, 2, 1, 3).reshape(-1, 8, 128)


def rows_of(tiles, count):
    return tiles.reshape(count // 8, -1, 8, 128).transpose(0, 2, 1, 3).reshape(count, -1)


def kernel_call(body, shapes, *args, smem=0):
    specs = [pl.BlockSpec(memory_space=pltpu.SMEM)] * smem + [pl.BlockSpec(memory_space=pltpu.VMEM)] * (len(args) - smem)
    return pl.pallas_call(
        body,
        out_shape=[jax.ShapeDtypeStruct(shape, jnp.float32) for shape in shapes],
        in_specs=specs,
        out_specs=[pl.BlockSpec(memory_space=pltpu.VMEM)] * len(shapes),
        compiler_params=pltpu.CompilerParams(vmem_limit_bytes=24 * 1024 * 1024),
    )(*args)


def shards(
    features,
    velocity,
    velocity_cot,
    surface_cot,
    damping,
    wet_mask,
    aggregate_map,
    coarse_inverse,
    conv_weight,
    conv_bias,
    out_weight,
    level_weight,
):
    f32 = jnp.float32
    n_lon, n_lat = lax.axis_size(LON), lax.axis_size(LAT)
    lon, lat = lax.axis_index(LON), lax.axis_index(LAT)
    n_layer, n_depth = lax.axis_size(LAYER), lax.axis_size(DEPTH)
    rank = lax.axis_index(LAYER)
    slot = rank % 16
    place = (slot * AGG).astype(jnp.int32)
    spot = jnp.where(slot < 8, 64, 0)

    single = jnp.concatenate([features.astype(f32), velocity, velocity_cot], axis=0)
    inner = features.astype(f32)
    several = jnp.stack([surface_cot, damping, wet_mask.astype(f32), aggregate_map.astype(f32)])
    n_single, n_several = single.shape[0], several.shape[0]
    coarse = tiles_of(coarse_inverse)

    def side_tiles(line, block):
        edge = jnp.concatenate([line, block.transpose(0, 2, 1).reshape(-1, CLON)], axis=0)
        edge = jnp.pad(edge, ((0, 64 - edge.shape[0]), (0, 0))).reshape(1, 8, 128)
        return jnp.concatenate([coarse, edge], axis=0)

    forward, backward = shifted(single, LAT, False)
    left = lax.ppermute(side_tiles(single[:, :, -1], several[:, :, -HALO:]), LAT, forward)
    right = lax.ppermute(side_tiles(single[:, :, 0], several[:, :, :HALO]), LAT, backward)

    local = restricted(surface_cot, aggregate_map.astype(f32), place)

    def merged(got):
        lane_slot = jnp.arange(128)[None, None] // AGG
        kept = jnp.where(lane_slot == jnp.arange(16)[None, :, None], got.reshape(-1, 16, 128), 0.0)
        return jnp.sum(kept, axis=1)

    def to_all(block, axes):
        return exchange(jnp.broadcast_to(block[None], (lax.axis_size(axes),) + block.shape), axes)

    row = merged(to_all(local, LAYER))
    row, left, right = lax.optimization_barrier((row, left, right))

    def unpack(tiles):
        edge = tiles[-1].reshape(64, CLON)
        block = edge[n_single : n_single + n_several * HALO].reshape(n_several, HALO, CLON)
        return tiles[:-1], edge[:n_single], block.transpose(0, 2, 1)

    coarse_left, line_left, block_left = unpack(left)
    coarse_right, line_right, block_right = unpack(right)
    band = jnp.concatenate([coarse_left, coarse, coarse_right], axis=0)
    several = ring_lanes(several, block_right, block_left)

    def end_tiles(at, second, block):
        line = ring_lanes(single[:, at, :], line_right[:, at : at + 1], line_left[:, at : at + 1])
        more = ring_lanes(
            inner[:, second, :], line_right[:CIN, second : second + 1], line_left[:CIN, second : second + 1]
        )
        edge = jnp.concatenate([line, block.reshape(-1, LANES), more], axis=0)
        edge = jnp.pad(edge, ((0, 96 - edge.shape[0]), (0, 0)))
        return jnp.concatenate([band, tiles_of(edge)], axis=0)

    forward, backward = shifted(single, LON, True)
    above = lax.ppermute(end_tiles(CLON - 1, CLON - 2, several[:, -HALO:]), LON, forward)
    below = lax.ppermute(end_tiles(0, 1, several[:, :HALO]), LON, backward)
    gathered = to_all(row, DEPTH).reshape(-1, 128)
    gathered, above, below = lax.optimization_barrier((gathered, above, below))

    count = band.shape[0]

    def unpack_rows(tiles):
        edge = rows_of(tiles[count:], 96)
        last = n_single + n_several * HALO
        block = edge[n_single:last].reshape(n_several, HALO, LANES)
        return tiles[:count], edge[:n_single], block, edge[last : last + CIN]

    band_above, line_above, block_above, more_above = unpack_rows(above)
    band_below, line_below, block_below, more_below = unpack_rows(below)
    fields = ring_rows(several, block_below, block_above)

    def unringed(line):
        return jnp.concatenate([line[:, -1:], line[:, : CLAT + 1]], axis=1)[:, None]

    def padded(first, last):
        def ends(line):
            return unringed(line[first:last])

        middle = jnp.concatenate(
            [line_left[first:last, :, None], single[first:last], line_right[first:last, :, None]], axis=2
        )
        return jnp.concatenate([ends(line_above), middle, ends(line_below)], axis=1)

    levels = velocity.shape[0]
    feat_pad = jnp.concatenate([unringed(more_above), padded(0, CIN), unringed(more_below)], axis=1).astype(jnp.bfloat16)
    vel_pad = padded(CIN, CIN + levels)
    cot_pad = padded(CIN + levels, CIN + 2 * levels)

    w, force, z, row, sums = kernel_call(
        solve_first,
        [(ROWS, LANES), (ROWS, LANES), (CLON, CLAT), (1, 128), (1, 128)],
        place[None],
        gathered,
        band,
        band_below,
        band_above,
        fields,
        smem=1,
    )

    around = patches_of(feat_pad)
    hidden = jnp.tanh(jnp.dot(conv_weight, around, preferred_element_type=f32) + conv_bias[:, None])
    logits = jnp.sum(out_weight[:, None] * hidden, axis=0).reshape(CLON + 2, CLAT)
    visc_rows = jax.nn.softplus(logits)
    logits, viscosity = logits[1:-1], visc_rows[1:-1]
    columns, hidden = around[:, CLAT:-CLAT], hidden[:, CLAT:-CLAT]

    to = jnp.arange(n_layer)[:, None]
    before, after = (to == rank - 1) & (lat > 0), (to == rank + 1) & (lat < n_lat - 1)

    def at_spot(line):
        line = jnp.pad(line, (0, 64 - CLON))
        blank = jnp.zeros_like(line)
        return jnp.where(spot > 0, jnp.concatenate([blank, line]), jnp.concatenate([line, blank]))[None]

    edge = jnp.where(after, at_spot(viscosity[:, -1]), 0.0) + jnp.where(before, at_spot(viscosity[:, 0]), 0.0)
    got = exchange((row + edge)[:, None], LAYER)

    def from_spot(mask):
        line = jnp.sum(jnp.where(mask, got[:, 0], 0.0), axis=0)
        return jnp.where(spot > 0, line[64 : 64 + CLON], line[:CLON])[:, None]

    visc_left, visc_right = from_spot(before), from_spot(after)
    gathered = to_all(merged(got), DEPTH).reshape(-1, 128)
    visc_above, visc_below = visc_rows[:1], visc_rows[-1:]

    def rim(line):
        return jnp.pad(line, ((0, 0), (0, LANES - CLAT)))

    visc = ring_rows(ring_lanes(viscosity, visc_right, visc_left), rim(visc_below), rim(visc_above))
    visc_pad = jnp.concatenate([visc[-1:], visc[: CLON + 1]], axis=0)
    visc_pad = jnp.concatenate([visc_pad[:, -1:], visc_pad[:, : CLAT + 1]], axis=1)

    lane = jnp.arange(LANES)[None]
    valid = jnp.where(lane < CLAT, 1.0, jnp.where(lane < CLAT + LANES // 4, lat < n_lat - 1, lat > 0).astype(f32))

    level = level_weight[:, None, None]
    base = jnp.zeros_like(velocity_cot)
    first = jnp.zeros_like(viscosity)
    slopes = []
    for visc_side, vel_side, cot_side in zip(neighbours(visc_pad), neighbours(vel_pad), neighbours(cot_pad)):
        change = cot_side - velocity_cot
        slope = vel_side - velocity
        base = base + 0.5 * (viscosity + visc_side)[None] * change
        first = first + jnp.sum(slope * change, axis=0)
        slopes.append(jnp.sum(level * slope, axis=0))
    base = velocity_cot + time_step * base
    cells_all = CLON * CLAT * n_lon * n_lat
    weight = jax.nn.sigmoid(logits) * (-0.5 * time_step / math.sqrt(cells_all))

    grads, spreads, sums = kernel_call(
        solve_second,
        [(3, CLON, CLAT), (2, CLON, CLAT), (1, 128)],
        gathered,
        band,
        band_below,
        band_above,
        fields,
        w,
        force,
        visc,
        valid,
        weight,
        jnp.stack(slopes),
        first,
        sums,
    )

    lines = grads.reshape(3, 1, CLON * CLAT)
    out_grad = jnp.sum(hidden[None] * lines, axis=2)
    pre = lines * (out_weight[:, None] * (1.0 - hidden * hidden))[None]
    bias_grad = jnp.sum(pre, axis=2)
    rounded = lax.reduce_precision(pre, 8, 7)
    high = rounded.astype(jnp.bfloat16)
    low = (pre - rounded).astype(jnp.bfloat16)

    def against(part):
        return lax.dot_general(
            part.reshape(3 * HID, -1), columns, (((1,), (1,)), ((), ())), preferred_element_type=f32
        )

    weight_grad = (against(high) + against(low)).reshape(3, HID, TAPS)
    rest = jnp.concatenate([weight_grad[..., 256:], bias_grad[..., None], out_grad[..., None]], axis=2)
    table = jnp.concatenate(
        [weight_grad[k, :, :256] for k in range(3)]
        + [rest[k] for k in range(3)]
        + [jnp.broadcast_to(sums[:, : 128 - 3 * SPARE], (HID, 128 - 3 * SPARE))],
        axis=1,
    )
    each = HID // n_layer
    part = jnp.sum(exchange(table.reshape(n_layer, each, table.shape[1]), LAYER), axis=0)
    mine, spread = kernel_call(finish, [(each, 384), (CLON, CLAT)], to_all(part, DEPTH), spreads)
    final = to_all(mine, LAYER).reshape(HID, 384)
    grad_velocity = base + level * spread[None]
    return (grad_velocity, final[:, :TAPS], final[:, TAPS], final[:, TAPS + 1])


def solution(mesh):
    n_lon, n_lat = mesh.shape["lon"], mesh.shape["lat"]
    y = min(8, n_lon // 2)
    shape = (n_lon // y, y, n_lat // 2, 2)
    grid = Mesh(np.asarray(mesh.devices).reshape(shape), LON + LAT)
    tile = P(None, LON, LAT)
    flat = P(LON, LAT)
    in_specs = (tile, tile, tile, flat, flat, flat, flat, P(LON + LAT, None), P(), P(), P(), P())
    out_specs = (tile, P(), P(), P())
    return jax.shard_map(shards, mesh=grid, in_specs=in_specs, out_specs=out_specs, check_vma=False)
```

```python
import math

import jax
import jax.numpy as jnp
import numpy as np
from jax import lax
from jax.experimental import pallas as pl
from jax.experimental.pallas import tpu as pltpu
from jax.sharding import Mesh
from jax.sharding import PartitionSpec as P

CIN = 32
HID = 64
AGG = 8
CNT = 256
TAPS = 9 * CIN
time_step = 0.1

CLON = 16
CLAT = 128
HALO = 3
ROWS = 24
LANES = 256
LON = ("z", "y")
LAT = ("x", "c")
LAYER = ("y", "x", "c")
DEPTH = ("z",)
SPARE = 34


def exchange(values, axes):
    return lax.all_to_all(values, axes, 0, 0, tiled=True)


def shifted(block, axes, periodic):
    count = lax.axis_size(axes)
    forward = [(i, i + 1) for i in range(count - 1)]
    if periodic:
        forward.append((count - 1, 0))
    return forward, [(target, source) for source, target in forward]


def ring_lanes(own, right, left):
    gap = LANES - CLAT - right.shape[-1] - left.shape[-1]
    return jnp.concatenate([own, right, jnp.zeros(own.shape[:-1] + (gap,), own.dtype), left], axis=-1)


def ring_rows(own, below, above):
    gap = ROWS - CLON - below.shape[-2] - above.shape[-2]
    shape = own.shape[:-2] + (gap, own.shape[-1])
    return jnp.concatenate([own, below, jnp.zeros(shape, own.dtype), above], axis=-2)


def roll(value, shift, axis):
    return pltpu.roll(value, shift % value.shape[axis], axis)


def sides(value):
    return (roll(value, -1, 0), roll(value, 1, 0), roll(value, -1, 1), roll(value, 1, 1))


def side_sum(value):
    a, b, c, d = sides(value)
    return (a + b) + (c + d)


def coarse_column(tiles, start, vector):
    acc = tiles[start] * vector[0:1]
    for k in range(1, vector.shape[0]):
        acc = acc + tiles[start + k] * vector[k : k + 1]
    return jnp.sum(acc, axis=1, keepdims=True)


def coarse_columns(gathered, left, coarse, right, above, below):
    vector = gathered[...]
    count = vector.shape[0]
    middle = [coarse_column(tiles, 0, vector) for tiles in (left, coarse, right)]
    outer = [[coarse_column(tiles, k * count, vector) for k in range(3)] for tiles in (above, below)]
    return outer[0], middle, outer[1]


def ring_fields(gathered, inner, above, below):
    start = 3 * gathered.shape[0]
    row = lax.broadcasted_iota(jnp.int32, (8, LANES), 0)
    out = []
    for k in range(inner.shape[0]):
        at = start + 2 * k
        low = jnp.concatenate([below[at], below[at + 1]], axis=1)
        high = jnp.concatenate([above[at], above[at + 1]], axis=1)
        out.append(jnp.concatenate([inner[k], jnp.where(row < 4, low, high)], axis=0))
    return out


def coarse_field(agg, above, middle, below):
    lane = lax.broadcasted_iota(jnp.int32, (1, CLAT), 1)
    row = lax.broadcasted_iota(jnp.int32, (ROWS - CLON, LANES), 0)

    def across(columns, k):
        left, own, right = (column[k : k + 1] for column in columns)
        side = jnp.where(lane < CLAT // 2, right, left)
        return jnp.concatenate([jnp.broadcast_to(own, (1, CLAT)), side], axis=1)

    field = jnp.zeros((ROWS, LANES), jnp.float32)
    for k in range(AGG):
        inner = jnp.broadcast_to(across(middle, k), (CLON, LANES))
        outer = jnp.where(row < (ROWS - CLON) // 2, across(below, k), across(above, k))
        field = jnp.where(agg == float(k), jnp.concatenate([inner, outer], axis=0), field)
    return field


def total(value):
    return jnp.sum(jnp.sum(value, axis=0, keepdims=True), axis=1, keepdims=True)


def restricted(value, agg, first):
    parts = [jnp.sum(jnp.where(agg == float(k), value, 0.0), axis=0, keepdims=True) for k in range(AGG)]
    sums = jnp.sum(jnp.concatenate(parts, axis=0), axis=1, keepdims=True) * (1.0 / math.sqrt(CNT))
    lane = lax.broadcasted_iota(jnp.int32, (AGG, 128), 1)
    row = lax.broadcasted_iota(jnp.int32, (AGG, 128), 0)
    return jnp.sum(jnp.where(lane == first + row, sums, 0.0), axis=0, keepdims=True)


def solve_first(place, gathered, left, coarse, right, above, below, inner, valid_ref, w_ref, f_ref, row_ref, sum_ref):
    rhs, damp, wet, agg = ring_fields(gathered, inner, above, below)
    diagonal = 4.0 + damp
    columns = coarse_columns(gathered, left, coarse, right, above, below)
    z = rhs / diagonal + coarse_field(agg, *columns)
    spread = side_sum(wet * z)
    w = diagonal * z - wet * spread
    w_ref[...] = w
    f_ref[...] = (spread - 4.0 * wet * z) * valid_ref[...]
    own = (slice(0, CLON), slice(0, CLAT))
    z_own, w_own = z[own], w[own]
    row_ref[...] = restricted(w_own, agg[own], place[0])
    lane = lax.broadcasted_iota(jnp.int32, (1, 128), 1)
    sum_ref[...] = jnp.where(lane == 0, total(rhs[own] * z_own), 0.0) + jnp.where(lane == 1, total(z_own * w_own), 0.0)


def solve_second(
    gathered, left, coarse, right, above, below, inner, valid_ref, w_ref, f_ref, weight_ref, slope_ref, first_ref,
    sum_in, grad_ref, force_ref, sum_ref,
):
    rhs, damp, wet, agg = ring_fields(gathered, inner, above, below)
    diagonal = 4.0 + damp
    w = w_ref[...]
    columns = coarse_columns(gathered, left, coarse, right, above, below)
    y = w / diagonal + coarse_field(agg, *columns)
    around = side_sum(wet * y)
    image = diagonal * y - wet * around
    own = (slice(0, CLON), slice(0, CLAT))
    y_own = y[own]
    lane = lax.broadcasted_iota(jnp.int32, (1, 128), 1)
    sums = sum_in[...]
    for at, value in ((2, rhs[own] * y_own), (3, w[own] * y_own), (4, y_own * image[own])):
        sums = sums + jnp.where(lane == at, total(value), 0.0)
    sum_ref[...] = sums
    weight = weight_ref[...]
    grad_ref[0] = first_ref[...] * weight
    second = (around - 4.0 * wet * y) * valid_ref[...]
    force_ref[...] = second
    for at, force in ((1, f_ref[...]), (2, second)):
        force_own = force[own]
        slope = jnp.zeros((CLON, CLAT), jnp.float32)
        for n, side in enumerate(sides(force)):
            slope = slope + slope_ref[n] * (side[own] - force_own)
        grad_ref[at] = slope * weight


def diffuse(visc_ref, first, second, spread_ref):
    own = (slice(0, CLON), slice(0, CLAT))
    visc = visc_ref[...]
    visc_sides = [0.5 * (visc[own] + side[own]) for side in sides(visc)]
    for at, force in ((0, first[...]), (1, second[...])):
        force_own = force[own]
        bend = jnp.zeros((CLON, CLAT), jnp.float32)
        for visc_side, side in zip(visc_sides, sides(force)):
            bend = bend + visc_side * (side[own] - force_own)
        spread_ref[at] = force_own + time_step * bend


def finish(parts, mine_ref, on_ref):
    row = jnp.sum(parts[...], axis=0)
    main, tail = 2 * 128, 6 * 128

    def scalar(k):
        at = tail + 3 * SPARE + k
        return row[:1, at : at + 1]

    e0, d0, cross, ww, g = (scalar(k) for k in range(5))
    step0 = e0 / d0
    e1 = e0 - step0 * d0 - step0 * cross + step0 * step0 * ww
    beta = e1 / e0
    lead = 1.0 + beta
    pw = lead * lead * d0 - 2.0 * lead * step0 * ww + step0 * step0 * g
    step1 = e1 / pw
    on_z = step0 + step1 * lead
    on_y = -step1 * step0
    front = row[:, :main] + on_z * row[:, main : 2 * main] + on_y * row[:, 2 * main : 3 * main]
    last = row[:, tail:]
    back = last + on_z * roll(last, -SPARE, 1) + on_y * roll(last, -2 * SPARE, 1)
    mine_ref[...] = jnp.concatenate([front, back], axis=1)
    lane = lax.broadcasted_iota(jnp.int32, (1, 128), 1)
    on_ref[...] = jnp.where(lane == 0, on_z, on_y)


def neighbours(padded):
    return (padded[..., 2:, 1:-1], padded[..., :-2, 1:-1], padded[..., 1:-1, 2:], padded[..., 1:-1, :-2])


def patches_of(block):
    rows = block.shape[-2] - 2
    width = block.shape[-1] - 2
    taps = [
        block[:, first : first + rows, second : second + width]
        for first in range(3)
        for second in range(3)
    ]
    return jnp.concatenate(taps, axis=0).reshape(-1, rows * width)


def tiles_of(rows):
    count, width = rows.shape
    return rows.reshape(count // 8, 8, width // 128, 128).transpose(0, 2, 1, 3).reshape(-1, 8, 128)


def rows_of(tiles, count):
    return tiles.reshape(count // 8, -1, 8, 128).transpose(0, 2, 1, 3).reshape(count, -1)


def kernel_call(body, shapes, *args, smem=0):
    specs = [pl.BlockSpec(memory_space=pltpu.SMEM)] * smem + [pl.BlockSpec(memory_space=pltpu.VMEM)] * (len(args) - smem)
    return pl.pallas_call(
        body,
        out_shape=[jax.ShapeDtypeStruct(shape, jnp.float32) for shape in shapes],
        in_specs=specs,
        out_specs=[pl.BlockSpec(memory_space=pltpu.VMEM)] * len(shapes),
        compiler_params=pltpu.CompilerParams(vmem_limit_bytes=24 * 1024 * 1024),
    )(*args)


def shards(
    features,
    velocity,
    velocity_cot,
    surface_cot,
    damping,
    wet_mask,
    aggregate_map,
    coarse_inverse,
    conv_weight,
    conv_bias,
    out_weight,
    level_weight,
):
    f32 = jnp.float32
    n_lon, n_lat = lax.axis_size(LON), lax.axis_size(LAT)
    lon, lat = lax.axis_index(LON), lax.axis_index(LAT)
    n_layer, n_depth = lax.axis_size(LAYER), lax.axis_size(DEPTH)
    rank = lax.axis_index(LAYER)
    slot = rank % 16
    place = (slot * AGG).astype(jnp.int32)

    single = jnp.concatenate([features.astype(f32), velocity, velocity_cot], axis=0)
    inner = features.astype(f32)
    several = jnp.stack([surface_cot, damping, wet_mask.astype(f32), aggregate_map.astype(f32)])
    n_single, n_several = single.shape[0], several.shape[0]
    coarse = tiles_of(coarse_inverse)

    whole_fields = several.reshape(-1, 8, 128)

    def side_tiles(line):
        edge = jnp.pad(line, ((0, 64 - line.shape[0]), (0, 0))).reshape(1, 8, 128)
        return jnp.concatenate([coarse, whole_fields, edge], axis=0)

    forward, backward = shifted(single, LAT, False)
    left = lax.ppermute(side_tiles(single[:, :, -1]), LAT, forward)
    right = lax.ppermute(side_tiles(single[:, :, 0]), LAT, backward)

    local = restricted(surface_cot, aggregate_map.astype(f32), place)

    def merged(got):
        lane_slot = jnp.arange(128)[None, None] // AGG
        kept = jnp.where(lane_slot == jnp.arange(16)[None, :, None], got.reshape(-1, 16, 128), 0.0)
        return jnp.sum(kept, axis=1)

    def to_all(block, axes):
        return exchange(jnp.broadcast_to(block[None], (lax.axis_size(axes),) + block.shape), axes)

    row = merged(to_all(local, LAYER))
    row, left, right = lax.optimization_barrier((row, left, right))

    count = coarse.shape[0]
    line_left = left[-1].reshape(64, CLON)[:n_single]
    line_right = right[-1].reshape(64, CLON)[:n_single]
    lane = jnp.arange(CLAT)[None, None]
    rest = jnp.where(lane < CLAT // 2, right[count:-1].reshape(several.shape), left[count:-1].reshape(several.shape))
    several = jnp.concatenate([several, rest], axis=2)
    band = jnp.concatenate([left[:count], coarse, right[:count]], axis=0)

    def end_tiles(at, second, block):
        line = ring_lanes(single[:, at, :], line_right[:, at : at + 1], line_left[:, at : at + 1])
        more = ring_lanes(
            inner[:, second, :], line_right[:CIN, second : second + 1], line_left[:CIN, second : second + 1]
        )
        edge = jnp.concatenate([block.reshape(-1, LANES), line, more], axis=0)
        return jnp.concatenate([band, tiles_of(edge)], axis=0)

    forward, backward = shifted(single, LON, True)
    above = lax.ppermute(end_tiles(CLON - 1, CLON - 2, several[:, -8:]), LON, forward)
    below = lax.ppermute(end_tiles(0, 1, several[:, :8]), LON, backward)
    gathered = to_all(row, DEPTH).reshape(-1, 128)
    gathered, above, below = lax.optimization_barrier((gathered, above, below))

    def unpack_rows(tiles):
        edge = rows_of(tiles[3 * count + 2 * n_several :], n_single + CIN)
        return edge[:n_single], edge[n_single:]

    line_above, more_above = unpack_rows(above)
    line_below, more_below = unpack_rows(below)
    lane = jnp.arange(LANES)[None]
    valid = jnp.where(lane < CLAT, 1.0, jnp.where(lane < CLAT + LANES // 4, lat < n_lat - 1, lat > 0).astype(f32))

    def unringed(line):
        return jnp.concatenate([line[:, -1:], line[:, : CLAT + 1]], axis=1)[:, None]

    def padded(first, last):
        def ends(line):
            return unringed(line[first:last])

        middle = jnp.concatenate(
            [line_left[first:last, :, None], single[first:last], line_right[first:last, :, None]], axis=2
        )
        return jnp.concatenate([ends(line_above), middle, ends(line_below)], axis=1)

    levels = velocity.shape[0]
    feat_pad = jnp.concatenate([unringed(more_above), padded(0, CIN), unringed(more_below)], axis=1).astype(jnp.bfloat16)
    vel_pad = padded(CIN, CIN + levels)
    cot_pad = padded(CIN + levels, CIN + 2 * levels)

    tiles = (left, coarse, right, above, below, several, valid)
    w, force, row, sums = kernel_call(
        solve_first, [(ROWS, LANES), (ROWS, LANES), (1, 128), (1, 128)], place[None], gathered, *tiles, smem=1
    )
    gathered = to_all(merged(to_all(row, LAYER)), DEPTH).reshape(-1, 128)

    around = patches_of(feat_pad)
    hidden = jnp.tanh(jnp.dot(conv_weight, around, preferred_element_type=f32) + conv_bias[:, None])
    logits = jnp.sum(out_weight[:, None] * hidden, axis=0).reshape(CLON + 2, CLAT)
    visc_rows = jax.nn.softplus(logits)
    logits, viscosity = logits[1:-1], visc_rows[1:-1]
    columns, hidden = around[:, CLAT:-CLAT], hidden[:, CLAT:-CLAT]

    level = level_weight[:, None, None]
    first = jnp.zeros_like(viscosity)
    slopes = []
    for vel_side, cot_side in zip(neighbours(vel_pad), neighbours(cot_pad)):
        slope = vel_side - velocity
        first = first + jnp.sum(slope * (cot_side - velocity_cot), axis=0)
        slopes.append(jnp.sum(level * slope, axis=0))
    cells_all = CLON * CLAT * n_lon * n_lat
    weight = jax.nn.sigmoid(logits) * (-0.5 * time_step / math.sqrt(cells_all))

    grads, second, sums = kernel_call(
        solve_second,
        [(3, CLON, CLAT), (ROWS, LANES), (1, 128)],
        gathered,
        *tiles,
        w,
        force,
        weight,
        jnp.stack(slopes),
        first,
        sums,
    )

    lines = grads.reshape(3, 1, CLON * CLAT)
    out_grad = jnp.sum(hidden[None] * lines, axis=2)
    pre = lines * (out_weight[:, None] * (1.0 - hidden * hidden))[None]
    bias_grad = jnp.sum(pre, axis=2)
    rounded = lax.reduce_precision(pre, 8, 7)
    high = rounded.astype(jnp.bfloat16)
    low = (pre - rounded).astype(jnp.bfloat16)

    def against(part):
        return lax.dot_general(
            part.reshape(3 * HID, -1), columns, (((1,), (1,)), ((), ())), preferred_element_type=f32
        )

    weight_grad = (against(high) + against(low)).reshape(3, HID, TAPS)
    each = HID // n_layer
    to = (jnp.arange(HID) // each)[:, None]
    edge = jnp.where((to == rank - 1) & (lat > 0), viscosity[None, :, 0], 0.0)
    edge = edge + jnp.where((to == rank + 1) & (lat < n_lat - 1), viscosity[None, :, -1], 0.0)
    edge = jnp.pad(edge, ((0, 0), (0, 128 - 3 * SPARE - 5 - CLON)))
    rest = jnp.concatenate([weight_grad[..., 256:], bias_grad[..., None], out_grad[..., None]], axis=2)
    table = jnp.concatenate(
        [weight_grad[k, :, :256] for k in range(3)]
        + [rest[k] for k in range(3)]
        + [jnp.broadcast_to(sums[:, :5], (HID, 5)), edge],
        axis=1,
    )
    got = exchange(table.reshape(n_layer, each, table.shape[1]), LAYER)
    part = jnp.sum(got, axis=0)
    mine, on = kernel_call(finish, [(each, 384), (1, 128)], to_all(part, DEPTH))

    to = jnp.arange(n_layer)[:, None]
    lines = got[:, 0, 6 * 128 + 3 * SPARE + 5 :][:, :CLON]
    visc_left = jnp.sum(jnp.where((to == rank - 1) & (lat > 0), lines, 0.0), axis=0)[:, None]
    visc_right = jnp.sum(jnp.where((to == rank + 1) & (lat < n_lat - 1), lines, 0.0), axis=0)[:, None]

    def rim(line):
        return jnp.pad(line, ((0, 0), (0, LANES - CLAT)))

    visc = ring_rows(ring_lanes(viscosity, visc_right, visc_left), rim(visc_rows[-1:]), rim(visc_rows[:1]))
    visc_pad = jnp.concatenate([visc[-1:], visc[: CLON + 1]], axis=0)
    visc_pad = jnp.concatenate([visc_pad[:, -1:], visc_pad[:, : CLAT + 1]], axis=1)
    (spreads,) = kernel_call(diffuse, [(2, CLON, CLAT)], visc, force, second)
    base = jnp.zeros_like(velocity_cot)
    for visc_side, cot_side in zip(neighbours(visc_pad), neighbours(cot_pad)):
        base = base + 0.5 * (viscosity + visc_side)[None] * (cot_side - velocity_cot)
    base = velocity_cot + time_step * base
    final = to_all(mine, LAYER).reshape(HID, 384)
    spread = on[:, :1] * spreads[0] + on[:, 1:2] * spreads[1]
    grad_velocity = base + level * spread[None]
    return (grad_velocity, final[:, :TAPS], final[:, TAPS], final[:, TAPS + 1])


def solution(mesh):
    n_lon, n_lat = mesh.shape["lon"], mesh.shape["lat"]
    y = min(8, n_lon // 2)
    shape = (n_lon // y, y, n_lat // 2, 2)
    grid = Mesh(np.asarray(mesh.devices).reshape(shape), LON + LAT)
    tile = P(None, LON, LAT)
    flat = P(LON, LAT)
    in_specs = (tile, tile, tile, flat, flat, flat, flat, P(LON + LAT, None), P(), P(), P(), P())
    out_specs = (tile, P(), P(), P())
    return jax.shard_map(shards, mesh=grid, in_specs=in_specs, out_specs=out_specs, check_vma=False)
```

```python
import math

import jax
import jax.numpy as jnp
import numpy as np
from jax import lax
from jax.experimental import pallas as pl
from jax.experimental.pallas import tpu as pltpu
from jax.sharding import Mesh
from jax.sharding import PartitionSpec as P

CIN = 32
HID = 64
AGG = 8
CNT = 256
TAPS = 9 * CIN
time_step = 0.1

CLON = 16
CLAT = 128
HALO = 3
ROWS = 24
LANES = 256
LON = ("z", "y")
LAT = ("x", "c")
LAYER = ("y", "x", "c")
DEPTH = ("z",)
SPARE = 34


def exchange(values, axes):
    return lax.all_to_all(values, axes, 0, 0, tiled=True)


def shifted(block, axes, periodic):
    count = lax.axis_size(axes)
    forward = [(i, i + 1) for i in range(count - 1)]
    if periodic:
        forward.append((count - 1, 0))
    return forward, [(target, source) for source, target in forward]


def ring_lanes(own, right, left):
    gap = LANES - CLAT - right.shape[-1] - left.shape[-1]
    return jnp.concatenate([own, right, jnp.zeros(own.shape[:-1] + (gap,), own.dtype), left], axis=-1)


def ring_rows(own, below, above):
    gap = ROWS - CLON - below.shape[-2] - above.shape[-2]
    shape = own.shape[:-2] + (gap, own.shape[-1])
    return jnp.concatenate([own, below, jnp.zeros(shape, own.dtype), above], axis=-2)


def roll(value, shift, axis):
    return pltpu.roll(value, shift % value.shape[axis], axis)


def sides(value):
    return (roll(value, -1, 0), roll(value, 1, 0), roll(value, -1, 1), roll(value, 1, 1))


def side_sum(value):
    a, b, c, d = sides(value)
    return (a + b) + (c + d)


def restrict_first(place, rhs, agg, row_ref):
    row = restricted(rhs[...], agg[...].astype(jnp.float32), place[0])
    row_ref[...] = jnp.broadcast_to(row[None], row_ref.shape)


def merge(got, out_ref):
    value = got[...].reshape(got.shape[0], 128)
    lane = lax.broadcasted_iota(jnp.int32, value.shape, 1)
    row = lax.broadcasted_iota(jnp.int32, value.shape, 0)
    value = jnp.where(lane // AGG == row % 16, value, 0.0)
    for k in range(out_ref.shape[1]):
        part = jnp.sum(value[16 * k : 16 * k + 16], axis=0, keepdims=True)
        for partner in range(out_ref.shape[0]):
            out_ref[partner, k : k + 1] = part


def add_parts(got, out_ref):
    part = jnp.sum(got[...], axis=0, keepdims=True)
    out_ref[...] = jnp.broadcast_to(part, out_ref.shape)


def coarse_column(tiles, start, vector):
    acc = tiles[start] * vector[0:1]
    for k in range(1, vector.shape[0]):
        acc = acc + tiles[start + k] * vector[k : k + 1]
    return jnp.sum(acc, axis=1, keepdims=True)


def coarse_columns(gathered, left, coarse, right, above, below):
    vector = gathered[...]
    count = vector.shape[0]
    middle = [coarse_column(tiles, 0, vector) for tiles in (left, coarse, right)]
    outer = [[coarse_column(tiles, k * count, vector) for k in range(3)] for tiles in (above, below)]
    return outer[0], middle, outer[1]


def ring_fields(gathered, inner, above, below):
    start = 3 * gathered.shape[0]
    row = lax.broadcasted_iota(jnp.int32, (8, LANES), 0)
    out = []
    for k in range(inner.shape[0]):
        at = start + 2 * k
        low = jnp.concatenate([below[at], below[at + 1]], axis=1)
        high = jnp.concatenate([above[at], above[at + 1]], axis=1)
        out.append(jnp.concatenate([inner[k], jnp.where(row < 4, low, high)], axis=0))
    return out


def coarse_field(agg, above, middle, below):
    lane = lax.broadcasted_iota(jnp.int32, (1, CLAT), 1)
    row = lax.broadcasted_iota(jnp.int32, (ROWS - CLON, LANES), 0)

    def across(columns, k):
        left, own, right = (column[k : k + 1] for column in columns)
        side = jnp.where(lane < CLAT // 2, right, left)
        return jnp.concatenate([jnp.broadcast_to(own, (1, CLAT)), side], axis=1)

    field = jnp.zeros((ROWS, LANES), jnp.float32)
    for k in range(AGG):
        inner = jnp.broadcast_to(across(middle, k), (CLON, LANES))
        outer = jnp.where(row < (ROWS - CLON) // 2, across(below, k), across(above, k))
        field = jnp.where(agg == float(k), jnp.concatenate([inner, outer], axis=0), field)
    return field


def total(value):
    return jnp.sum(jnp.sum(value, axis=0, keepdims=True), axis=1, keepdims=True)


def restricted(value, agg, first):
    parts = [jnp.sum(jnp.where(agg == float(k), value, 0.0), axis=0, keepdims=True) for k in range(AGG)]
    sums = jnp.sum(jnp.concatenate(parts, axis=0), axis=1, keepdims=True) * (1.0 / math.sqrt(CNT))
    lane = lax.broadcasted_iota(jnp.int32, (AGG, 128), 1)
    row = lax.broadcasted_iota(jnp.int32, (AGG, 128), 0)
    return jnp.sum(jnp.where(lane == first + row, sums, 0.0), axis=0, keepdims=True)


def solve_first(place, gathered, left, coarse, right, above, below, inner, valid_ref, w_ref, f_ref, row_ref, sum_ref):
    rhs, damp, wet, agg = ring_fields(gathered, inner, above, below)
    diagonal = 4.0 + damp
    columns = coarse_columns(gathered, left, coarse, right, above, below)
    z = rhs / diagonal + coarse_field(agg, *columns)
    spread = side_sum(wet * z)
    w = diagonal * z - wet * spread
    w_ref[...] = w
    f_ref[...] = (spread - 4.0 * wet * z) * valid_ref[...]
    own = (slice(0, CLON), slice(0, CLAT))
    z_own, w_own = z[own], w[own]
    row = restricted(w_own, agg[own], place[0])
    row_ref[...] = jnp.broadcast_to(row[None], row_ref.shape)
    lane = lax.broadcasted_iota(jnp.int32, (1, 128), 1)
    sum_ref[...] = jnp.where(lane == 0, total(rhs[own] * z_own), 0.0) + jnp.where(lane == 1, total(z_own * w_own), 0.0)


def solve_second(
    gathered, left, coarse, right, above, below, inner, valid_ref, w_ref, f_ref, weight_ref, slope_ref, first_ref,
    sum_in, grad_ref, force_ref, sum_ref,
):
    rhs, damp, wet, agg = ring_fields(gathered, inner, above, below)
    diagonal = 4.0 + damp
    w = w_ref[...]
    columns = coarse_columns(gathered, left, coarse, right, above, below)
    y = w / diagonal + coarse_field(agg, *columns)
    around = side_sum(wet * y)
    image = diagonal * y - wet * around
    own = (slice(0, CLON), slice(0, CLAT))
    y_own = y[own]
    lane = lax.broadcasted_iota(jnp.int32, (1, 128), 1)
    sums = sum_in[...]
    for at, value in ((2, rhs[own] * y_own), (3, w[own] * y_own), (4, y_own * image[own])):
        sums = sums + jnp.where(lane == at, total(value), 0.0)
    sum_ref[...] = sums
    weight = weight_ref[...]
    grad_ref[0] = first_ref[...] * weight
    second = (around - 4.0 * wet * y) * valid_ref[...]
    force_ref[...] = second
    for at, force in ((1, f_ref[...]), (2, second)):
        force_own = force[own]
        slope = jnp.zeros((CLON, CLAT), jnp.float32)
        for n, side in enumerate(sides(force)):
            slope = slope + slope_ref[n] * (side[own] - force_own)
        grad_ref[at] = slope * weight


def diffuse(visc_ref, first, second, spread_ref):
    own = (slice(0, CLON), slice(0, CLAT))
    visc = visc_ref[...]
    visc_sides = [0.5 * (visc[own] + side[own]) for side in sides(visc)]
    for at, force in ((0, first[...]), (1, second[...])):
        force_own = force[own]
        bend = jnp.zeros((CLON, CLAT), jnp.float32)
        for visc_side, side in zip(visc_sides, sides(force)):
            bend = bend + visc_side * (side[own] - force_own)
        spread_ref[at] = force_own + time_step * bend


def finish(parts, mine_ref, on_ref):
    row = jnp.sum(parts[...], axis=0)
    main, tail = 2 * 128, 6 * 128

    def scalar(k):
        at = tail + 3 * SPARE + k
        return row[:1, at : at + 1]

    e0, d0, cross, ww, g = (scalar(k) for k in range(5))
    step0 = e0 / d0
    e1 = e0 - step0 * d0 - step0 * cross + step0 * step0 * ww
    beta = e1 / e0
    lead = 1.0 + beta
    pw = lead * lead * d0 - 2.0 * lead * step0 * ww + step0 * step0 * g
    step1 = e1 / pw
    on_z = step0 + step1 * lead
    on_y = -step1 * step0
    front = row[:, :main] + on_z * row[:, main : 2 * main] + on_y * row[:, 2 * main : 3 * main]
    last = row[:, tail:]
    back = last + on_z * roll(last, -SPARE, 1) + on_y * roll(last, -2 * SPARE, 1)
    mine = jnp.concatenate([front, back], axis=1)
    mine_ref[...] = jnp.broadcast_to(mine[None], mine_ref.shape)
    lane = lax.broadcasted_iota(jnp.int32, (1, 128), 1)
    on_ref[...] = jnp.where(lane == 0, on_z, on_y)


def neighbours(padded):
    return (padded[..., 2:, 1:-1], padded[..., :-2, 1:-1], padded[..., 1:-1, 2:], padded[..., 1:-1, :-2])


def patches_of(block):
    rows = block.shape[-2] - 2
    width = block.shape[-1] - 2
    taps = [
        block[:, first : first + rows, second : second + width]
        for first in range(3)
        for second in range(3)
    ]
    return jnp.concatenate(taps, axis=0).reshape(-1, rows * width)


def tiles_of(rows):
    count, width = rows.shape
    return rows.reshape(count // 8, 8, width // 128, 128).transpose(0, 2, 1, 3).reshape(-1, 8, 128)


def rows_of(tiles, count):
    return tiles.reshape(count // 8, -1, 8, 128).transpose(0, 2, 1, 3).reshape(count, -1)


def kernel_call(body, shapes, *args, smem=0):
    specs = [pl.BlockSpec(memory_space=pltpu.SMEM)] * smem + [pl.BlockSpec(memory_space=pltpu.VMEM)] * (len(args) - smem)
    return pl.pallas_call(
        body,
        out_shape=[jax.ShapeDtypeStruct(shape, jnp.float32) for shape in shapes],
        in_specs=specs,
        out_specs=[pl.BlockSpec(memory_space=pltpu.VMEM)] * len(shapes),
        compiler_params=pltpu.CompilerParams(vmem_limit_bytes=24 * 1024 * 1024),
    )(*args)


def shards(
    features,
    velocity,
    velocity_cot,
    surface_cot,
    damping,
    wet_mask,
    aggregate_map,
    coarse_inverse,
    conv_weight,
    conv_bias,
    out_weight,
    level_weight,
):
    f32 = jnp.float32
    n_lon, n_lat = lax.axis_size(LON), lax.axis_size(LAT)
    lon, lat = lax.axis_index(LON), lax.axis_index(LAT)
    n_layer, n_depth = lax.axis_size(LAYER), lax.axis_size(DEPTH)
    rank = lax.axis_index(LAYER)
    slot = rank % 16
    place = (slot * AGG).astype(jnp.int32)

    single = jnp.concatenate([features.astype(f32), velocity, velocity_cot], axis=0)
    inner = features.astype(f32)
    several = jnp.stack([surface_cot, damping, wet_mask.astype(f32), aggregate_map.astype(f32)])
    n_single, n_several = single.shape[0], several.shape[0]
    coarse = tiles_of(coarse_inverse)

    whole_fields = several.reshape(-1, 8, 128)

    def side_tiles(line):
        edge = jnp.pad(line, ((0, 64 - line.shape[0]), (0, 0))).reshape(1, 8, 128)
        return jnp.concatenate([coarse, whole_fields, edge], axis=0)

    forward, backward = shifted(single, LAT, False)
    left = lax.ppermute(side_tiles(single[:, :, -1]), LAT, forward)
    right = lax.ppermute(side_tiles(single[:, :, 0]), LAT, backward)

    every = (n_layer, 1, 128)
    dense = (n_depth, n_layer * AGG // 128, 128)
    (local,) = kernel_call(restrict_first, [every], place[None], surface_cot, aggregate_map, smem=1)

    (row,) = kernel_call(merge, [dense], exchange(local, LAYER))
    row, left, right = lax.optimization_barrier((row, left, right))

    count = coarse.shape[0]
    line_left = left[-1].reshape(64, CLON)[:n_single]
    line_right = right[-1].reshape(64, CLON)[:n_single]
    lane = jnp.arange(CLAT)[None, None]
    rest = jnp.where(lane < CLAT // 2, right[count:-1].reshape(several.shape), left[count:-1].reshape(several.shape))
    several = jnp.concatenate([several, rest], axis=2)
    band = jnp.concatenate([left[:count], coarse, right[:count]], axis=0)

    def end_tiles(at, second, block):
        line = ring_lanes(single[:, at, :], line_right[:, at : at + 1], line_left[:, at : at + 1])
        more = ring_lanes(
            inner[:, second, :], line_right[:CIN, second : second + 1], line_left[:CIN, second : second + 1]
        )
        edge = jnp.concatenate([block.reshape(-1, LANES), line, more], axis=0)
        return jnp.concatenate([band, tiles_of(edge)], axis=0)

    forward, backward = shifted(single, LON, True)
    above = lax.ppermute(end_tiles(CLON - 1, CLON - 2, several[:, -8:]), LON, forward)
    below = lax.ppermute(end_tiles(0, 1, several[:, :8]), LON, backward)
    gathered = exchange(row, DEPTH).reshape(-1, 128)
    gathered, above, below = lax.optimization_barrier((gathered, above, below))

    def unpack_rows(tiles):
        edge = rows_of(tiles[3 * count + 2 * n_several :], n_single + CIN)
        return edge[:n_single], edge[n_single:]

    line_above, more_above = unpack_rows(above)
    line_below, more_below = unpack_rows(below)
    lane = jnp.arange(LANES)[None]
    valid = jnp.where(lane < CLAT, 1.0, jnp.where(lane < CLAT + LANES // 4, lat < n_lat - 1, lat > 0).astype(f32))

    def unringed(line):
        return jnp.concatenate([line[:, -1:], line[:, : CLAT + 1]], axis=1)[:, None]

    def padded(first, last, line_left, line_right):
        def ends(line):
            return unringed(line[first:last])

        middle = jnp.concatenate(
            [line_left[first:last, :, None], single[first:last], line_right[first:last, :, None]], axis=2
        )
        return jnp.concatenate([ends(line_above), middle, ends(line_below)], axis=1)

    tiles = (left, coarse, right, above, below, several, valid)
    w, force, row, sums = kernel_call(
        solve_first, [(ROWS, LANES), (ROWS, LANES), every, (1, 128)], place[None], gathered, *tiles, smem=1
    )
    row, line_left, line_right = lax.optimization_barrier((row, line_left, line_right))
    feat_pad = jnp.concatenate(
        [unringed(more_above), padded(0, CIN, line_left, line_right), unringed(more_below)], axis=1
    ).astype(jnp.bfloat16)
    (row,) = kernel_call(merge, [dense], exchange(row, LAYER))
    row, line_left, line_right = lax.optimization_barrier((row, line_left, line_right))
    levels = velocity.shape[0]
    vel_pad = padded(CIN, CIN + levels, line_left, line_right)
    cot_pad = padded(CIN + levels, CIN + 2 * levels, line_left, line_right)
    gathered = exchange(row, DEPTH).reshape(-1, 128)

    around = patches_of(feat_pad)
    hidden = jnp.tanh(jnp.dot(conv_weight, around, preferred_element_type=f32) + conv_bias[:, None])
    logits = jnp.sum(out_weight[:, None] * hidden, axis=0).reshape(CLON + 2, CLAT)
    visc_rows = jax.nn.softplus(logits)
    logits, viscosity = logits[1:-1], visc_rows[1:-1]
    columns, hidden = around[:, CLAT:-CLAT], hidden[:, CLAT:-CLAT]

    level = level_weight[:, None, None]
    first = jnp.zeros_like(viscosity)
    slopes = []
    for vel_side, cot_side in zip(neighbours(vel_pad), neighbours(cot_pad)):
        slope = vel_side - velocity
        first = first + jnp.sum(slope * (cot_side - velocity_cot), axis=0)
        slopes.append(jnp.sum(level * slope, axis=0))
    cells_all = CLON * CLAT * n_lon * n_lat
    weight = jax.nn.sigmoid(logits) * (-0.5 * time_step / math.sqrt(cells_all))

    grads, second, sums = kernel_call(
        solve_second,
        [(3, CLON, CLAT), (ROWS, LANES), (1, 128)],
        gathered,
        *tiles,
        w,
        force,
        weight,
        jnp.stack(slopes),
        first,
        sums,
    )

    lines = grads.reshape(3, 1, CLON * CLAT)
    out_grad = jnp.sum(hidden[None] * lines, axis=2)
    pre = lines * (out_weight[:, None] * (1.0 - hidden * hidden))[None]
    bias_grad = jnp.sum(pre, axis=2)
    rounded = lax.reduce_precision(pre, 8, 7)
    high = rounded.astype(jnp.bfloat16)
    low = (pre - rounded).astype(jnp.bfloat16)

    def against(part):
        return lax.dot_general(
            part.reshape(3 * HID, -1), columns, (((1,), (1,)), ((), ())), preferred_element_type=f32
        )

    weight_grad = (against(high) + against(low)).reshape(3, HID, TAPS)
    each = HID // n_layer
    to = (jnp.arange(HID) // each)[:, None]
    edge = jnp.where((to == rank - 1) & (lat > 0), viscosity[None, :, 0], 0.0)
    edge = edge + jnp.where((to == rank + 1) & (lat < n_lat - 1), viscosity[None, :, -1], 0.0)
    edge = jnp.pad(edge, ((0, 0), (0, 128 - 3 * SPARE - 5 - CLON)))
    rest = jnp.concatenate([weight_grad[..., 256:], bias_grad[..., None], out_grad[..., None]], axis=2)
    table = jnp.concatenate(
        [weight_grad[k, :, :256] for k in range(3)]
        + [rest[k] for k in range(3)]
        + [jnp.broadcast_to(sums[:, :5], (HID, 5)), edge],
        axis=1,
    )
    got = exchange(table.reshape(n_layer, each, table.shape[1]), LAYER)
    (part,) = kernel_call(add_parts, [(n_depth, each, table.shape[1])], got)
    mine, on = kernel_call(finish, [(n_layer, each, 384), (1, 128)], exchange(part, DEPTH))

    to = jnp.arange(n_layer)[:, None]
    lines = got[:, 0, 6 * 128 + 3 * SPARE + 5 :][:, :CLON]
    visc_left = jnp.sum(jnp.where((to == rank - 1) & (lat > 0), lines, 0.0), axis=0)[:, None]
    visc_right = jnp.sum(jnp.where((to == rank + 1) & (lat < n_lat - 1), lines, 0.0), axis=0)[:, None]

    def rim(line):
        return jnp.pad(line, ((0, 0), (0, LANES - CLAT)))

    visc = ring_rows(ring_lanes(viscosity, visc_right, visc_left), rim(visc_rows[-1:]), rim(visc_rows[:1]))
    visc_pad = jnp.concatenate([visc[-1:], visc[: CLON + 1]], axis=0)
    visc_pad = jnp.concatenate([visc_pad[:, -1:], visc_pad[:, : CLAT + 1]], axis=1)
    (spreads,) = kernel_call(diffuse, [(2, CLON, CLAT)], visc, force, second)
    base = jnp.zeros_like(velocity_cot)
    for visc_side, cot_side in zip(neighbours(visc_pad), neighbours(cot_pad)):
        base = base + 0.5 * (viscosity + visc_side)[None] * (cot_side - velocity_cot)
    base = velocity_cot + time_step * base
    final = exchange(mine, LAYER).reshape(HID, 384)
    spread = on[:, :1] * spreads[0] + on[:, 1:2] * spreads[1]
    grad_velocity = base + level * spread[None]
    return (grad_velocity, final[:, :TAPS], final[:, TAPS], final[:, TAPS + 1])


def solution(mesh):
    n_lon, n_lat = mesh.shape["lon"], mesh.shape["lat"]
    y = min(8, n_lon // 2)
    shape = (n_lon // y, y, n_lat // 2, 2)
    grid = Mesh(np.asarray(mesh.devices).reshape(shape), LON + LAT)
    tile = P(None, LON, LAT)
    flat = P(LON, LAT)
    in_specs = (tile, tile, tile, flat, flat, flat, flat, P(LON + LAT, None), P(), P(), P(), P())
    out_specs = (tile, P(), P(), P())
    return jax.shard_map(shards, mesh=grid, in_specs=in_specs, out_specs=out_specs, check_vma=False)
```

```python
import math

import jax
import jax.numpy as jnp
import numpy as np
from jax import lax
from jax.experimental import pallas as pl
from jax.experimental.pallas import tpu as pltpu
from jax.sharding import Mesh
from jax.sharding import PartitionSpec as P

CIN = 32
HID = 64
AGG = 8
CNT = 256
TAPS = 9 * CIN
time_step = 0.1

CLON = 16
CLAT = 128
HALO = 3
ROWS = 24
LANES = 256
LON = ("z", "y")
LAT = ("x", "c")
LAYER = ("y", "x", "c")
DEPTH = ("z",)
SPARE = 34


def exchange(values, axes):
    return lax.all_to_all(values, axes, 0, 0, tiled=True)


def shifted(block, axes, periodic):
    count = lax.axis_size(axes)
    forward = [(i, i + 1) for i in range(count - 1)]
    if periodic:
        forward.append((count - 1, 0))
    return forward, [(target, source) for source, target in forward]


def ring_lanes(own, right, left):
    gap = LANES - CLAT - right.shape[-1] - left.shape[-1]
    return jnp.concatenate([own, right, jnp.zeros(own.shape[:-1] + (gap,), own.dtype), left], axis=-1)


def ring_rows(own, below, above):
    gap = ROWS - CLON - below.shape[-2] - above.shape[-2]
    shape = own.shape[:-2] + (gap, own.shape[-1])
    return jnp.concatenate([own, below, jnp.zeros(shape, own.dtype), above], axis=-2)


def roll(value, shift, axis):
    return pltpu.roll(value, shift % value.shape[axis], axis)


def sides(value):
    return (roll(value, -1, 0), roll(value, 1, 0), roll(value, -1, 1), roll(value, 1, 1))


def side_sum(value):
    a, b, c, d = sides(value)
    return (a + b) + (c + d)


def coarse_column(tiles, start, vector):
    acc = tiles[start] * vector[0:1]
    for k in range(1, vector.shape[0]):
        acc = acc + tiles[start + k] * vector[k : k + 1]
    return jnp.sum(acc, axis=1, keepdims=True)


def solve_start(rhs, damp, wet, agg, columns):
    diagonal = 4.0 + damp
    z = rhs / diagonal + coarse_field(agg, *columns)
    spread = side_sum(wet * z)
    return z, diagonal * z - wet * spread, spread - 4.0 * wet * z


def ring_fields(inner, low, high):
    row = lax.broadcasted_iota(jnp.int32, (8, LANES), 0)
    return [jnp.concatenate([inner[k], jnp.where(row < 4, low[k], high[k])], axis=0) for k in range(inner.shape[0])]


def coarse_field(agg, above, middle, below):
    lane = lax.broadcasted_iota(jnp.int32, (1, CLAT), 1)
    row = lax.broadcasted_iota(jnp.int32, (ROWS - CLON, LANES), 0)

    def across(columns, k):
        left, own, right = (column[k : k + 1] for column in columns)
        side = jnp.where(lane < CLAT // 2, right, left)
        return jnp.concatenate([jnp.broadcast_to(own, (1, CLAT)), side], axis=1)

    field = jnp.zeros((ROWS, LANES), jnp.float32)
    for k in range(AGG):
        inner = jnp.broadcast_to(across(middle, k), (CLON, LANES))
        outer = jnp.where(row < (ROWS - CLON) // 2, across(below, k), across(above, k))
        field = jnp.where(agg == float(k), jnp.concatenate([inner, outer], axis=0), field)
    return field


def total(value):
    return jnp.sum(jnp.sum(value, axis=0, keepdims=True), axis=1, keepdims=True)


def restricted(value, agg, first):
    parts = [jnp.sum(jnp.where(agg == float(k), value, 0.0), axis=0, keepdims=True) for k in range(AGG)]
    sums = jnp.sum(jnp.concatenate(parts, axis=0), axis=1, keepdims=True) * (1.0 / math.sqrt(CNT))
    lane = lax.broadcasted_iota(jnp.int32, (AGG, 128), 1)
    row = lax.broadcasted_iota(jnp.int32, (AGG, 128), 0)
    return jnp.sum(jnp.where(lane == first + row, sums, 0.0), axis=0, keepdims=True)


def solve_first(place, gathered, left, coarse, right, above, below, inner, row_ref, sum_ref):
    vector = gathered[...]
    count = vector.shape[0]

    def outer(tiles):
        blank = jnp.zeros((8, LANES - CLAT), jnp.float32)
        return [jnp.concatenate([tiles[count + k], blank], axis=1) for k in range(inner.shape[0])]

    rhs, damp, wet, agg = ring_fields(inner, outer(below), outer(above))
    none = jnp.zeros((AGG, 1), jnp.float32)
    middle = [coarse_column(tiles, 0, vector) for tiles in (left, coarse, right)]
    ends = [[none, coarse_column(tiles, 0, vector), none] for tiles in (above, below)]
    z, w, force = solve_start(rhs, damp, wet, agg, (ends[0], middle, ends[1]))
    own = (slice(0, CLON), slice(0, CLAT))
    z_own, w_own = z[own], w[own]
    row_ref[...] = restricted(w_own, agg[own], place[0])
    lane = lax.broadcasted_iota(jnp.int32, (1, 128), 1)
    sum_ref[...] = jnp.where(lane == 0, total(rhs[own] * z_own), 0.0) + jnp.where(lane == 1, total(z_own * w_own), 0.0)


def solve_second(
    gathered_first, gathered, left, coarse, right, above, below, far_above, far_below, inner, valid_ref, weight_ref,
    slope_ref, first_ref, sum_in, grad_ref, force_ref, sum_ref,
):
    count = gathered.shape[0]

    def outer(tiles):
        at = 2 * count
        return [
            jnp.concatenate([tiles[at + 2 * k], tiles[at + 2 * k + 1]], axis=1) for k in range(inner.shape[0])
        ]

    def columns_of(ref):
        vector = ref[...]
        middle = [coarse_column(tiles, 0, vector) for tiles in (left, coarse, right)]
        ends = [
            [coarse_column(far, 0, vector), coarse_column(near, 0, vector), coarse_column(far, count, vector)]
            for near, far in ((above, far_above), (below, far_below))
        ]
        return ends[0], middle, ends[1]

    rhs, damp, wet, agg = ring_fields(inner, outer(far_below), outer(far_above))
    diagonal = 4.0 + damp
    z, w, leading = solve_start(rhs, damp, wet, agg, columns_of(gathered_first))
    y = w / diagonal + coarse_field(agg, *columns_of(gathered))
    around = side_sum(wet * y)
    image = diagonal * y - wet * around
    own = (slice(0, CLON), slice(0, CLAT))
    y_own = y[own]
    lane = lax.broadcasted_iota(jnp.int32, (1, 128), 1)
    sums = sum_in[...]
    for at, value in ((2, rhs[own] * y_own), (3, w[own] * y_own), (4, y_own * image[own])):
        sums = sums + jnp.where(lane == at, total(value), 0.0)
    sum_ref[...] = sums
    weight = weight_ref[...]
    grad_ref[0] = first_ref[...] * weight
    forces = (leading * valid_ref[...], (around - 4.0 * wet * y) * valid_ref[...])
    for at, force in enumerate(forces, 1):
        force_ref[at - 1] = force
        force_own = force[own]
        slope = jnp.zeros((CLON, CLAT), jnp.float32)
        for n, side in enumerate(sides(force)):
            slope = slope + slope_ref[n] * (side[own] - force_own)
        grad_ref[at] = slope * weight


def diffuse(visc_ref, forces, spread_ref):
    own = (slice(0, CLON), slice(0, CLAT))
    visc = visc_ref[...]
    visc_sides = [0.5 * (visc[own] + side[own]) for side in sides(visc)]
    for at in range(2):
        force = forces[at]
        force_own = force[own]
        bend = jnp.zeros((CLON, CLAT), jnp.float32)
        for visc_side, side in zip(visc_sides, sides(force)):
            bend = bend + visc_side * (side[own] - force_own)
        spread_ref[at] = force_own + time_step * bend


def finish(parts, mine_ref, on_ref):
    row = jnp.sum(parts[...], axis=0)
    main, tail = 2 * 128, 6 * 128

    def scalar(k):
        at = tail + 3 * SPARE + k
        return row[:1, at : at + 1]

    e0, d0, cross, ww, g = (scalar(k) for k in range(5))
    step0 = e0 / d0
    e1 = e0 - step0 * d0 - step0 * cross + step0 * step0 * ww
    beta = e1 / e0
    lead = 1.0 + beta
    pw = lead * lead * d0 - 2.0 * lead * step0 * ww + step0 * step0 * g
    step1 = e1 / pw
    on_z = step0 + step1 * lead
    on_y = -step1 * step0
    front = row[:, :main] + on_z * row[:, main : 2 * main] + on_y * row[:, 2 * main : 3 * main]
    last = row[:, tail:]
    back = last + on_z * roll(last, -SPARE, 1) + on_y * roll(last, -2 * SPARE, 1)
    mine_ref[...] = jnp.concatenate([front, back], axis=1)
    lane = lax.broadcasted_iota(jnp.int32, (1, 128), 1)
    on_ref[...] = jnp.where(lane == 0, on_z, on_y)


def neighbours(padded):
    return (padded[..., 2:, 1:-1], padded[..., :-2, 1:-1], padded[..., 1:-1, 2:], padded[..., 1:-1, :-2])


def patches_of(block):
    rows = block.shape[-2] - 2
    width = block.shape[-1] - 2
    taps = [
        block[:, first : first + rows, second : second + width]
        for first in range(3)
        for second in range(3)
    ]
    return jnp.concatenate(taps, axis=0).reshape(-1, rows * width)


def tiles_of(rows):
    count, width = rows.shape
    return rows.reshape(count // 8, 8, width // 128, 128).transpose(0, 2, 1, 3).reshape(-1, 8, 128)


def rows_of(tiles, count):
    return tiles.reshape(count // 8, -1, 8, 128).transpose(0, 2, 1, 3).reshape(count, -1)


def kernel_call(body, shapes, *args, smem=0):
    specs = [pl.BlockSpec(memory_space=pltpu.SMEM)] * smem + [pl.BlockSpec(memory_space=pltpu.VMEM)] * (len(args) - smem)
    return pl.pallas_call(
        body,
        out_shape=[jax.ShapeDtypeStruct(shape, jnp.float32) for shape in shapes],
        in_specs=specs,
        out_specs=[pl.BlockSpec(memory_space=pltpu.VMEM)] * len(shapes),
        compiler_params=pltpu.CompilerParams(vmem_limit_bytes=24 * 1024 * 1024),
    )(*args)


def shards(
    features,
    velocity,
    velocity_cot,
    surface_cot,
    damping,
    wet_mask,
    aggregate_map,
    coarse_inverse,
    conv_weight,
    conv_bias,
    out_weight,
    level_weight,
):
    f32 = jnp.float32
    n_lon, n_lat = lax.axis_size(LON), lax.axis_size(LAT)
    lon, lat = lax.axis_index(LON), lax.axis_index(LAT)
    n_layer, n_depth = lax.axis_size(LAYER), lax.axis_size(DEPTH)
    rank = lax.axis_index(LAYER)
    slot = rank % 16
    place = (slot * AGG).astype(jnp.int32)

    single = jnp.concatenate([features.astype(f32), velocity, velocity_cot], axis=0)
    inner = features.astype(f32)
    several = jnp.stack([surface_cot, damping, wet_mask.astype(f32), aggregate_map.astype(f32)])
    n_single, n_several = single.shape[0], several.shape[0]
    coarse = tiles_of(coarse_inverse)

    whole_fields = several.reshape(-1, 8, 128)

    def side_tiles(line):
        edge = jnp.pad(line, ((0, 64 - line.shape[0]), (0, 0))).reshape(1, 8, 128)
        return jnp.concatenate([coarse, whole_fields, edge], axis=0)

    forward, backward = shifted(single, LAT, False)
    left = lax.ppermute(side_tiles(single[:, :, -1]), LAT, forward)
    right = lax.ppermute(side_tiles(single[:, :, 0]), LAT, backward)

    forward_lon, backward_lon = shifted(single, LON, True)
    above = lax.ppermute(jnp.concatenate([coarse, several[:, 8:]], axis=0), LON, forward_lon)
    below = lax.ppermute(jnp.concatenate([coarse, several[:, :8]], axis=0), LON, backward_lon)

    local = restricted(surface_cot, aggregate_map.astype(f32), place)

    def merged(got):
        lane_slot = jnp.arange(128)[None, None] // AGG
        kept = jnp.where(lane_slot == jnp.arange(16)[None, :, None], got.reshape(-1, 16, 128), 0.0)
        return jnp.sum(kept, axis=1)

    def to_all(block, axes):
        return exchange(jnp.broadcast_to(block[None], (lax.axis_size(axes),) + block.shape), axes)

    row = merged(to_all(local, LAYER))
    gathered_first = to_all(row, DEPTH).reshape(-1, 128)
    gathered_first, left, right, above, below = lax.optimization_barrier((gathered_first, left, right, above, below))

    count = coarse.shape[0]
    line_left = left[-1].reshape(64, CLON)[:n_single]
    line_right = right[-1].reshape(64, CLON)[:n_single]
    lane = jnp.arange(CLAT)[None, None]
    rest = jnp.where(lane < CLAT // 2, right[count:-1].reshape(several.shape), left[count:-1].reshape(several.shape))
    several = jnp.concatenate([several, rest], axis=2)
    row, sums = kernel_call(
        solve_first,
        [(1, 128), (1, 128)],
        place[None],
        gathered_first,
        left,
        coarse,
        right,
        above,
        below,
        several,
        smem=1,
    )
    row, line_left, line_right = lax.optimization_barrier((row, line_left, line_right))
    band = jnp.concatenate([left[:count], right[:count]], axis=0)

    def end_tiles(at, second, block):
        line = ring_lanes(single[:, at, :], line_right[:, at : at + 1], line_left[:, at : at + 1])
        more = ring_lanes(
            inner[:, second, :], line_right[:CIN, second : second + 1], line_left[:CIN, second : second + 1]
        )
        edge = jnp.concatenate([block.reshape(-1, LANES), line, more], axis=0)
        return jnp.concatenate([band, tiles_of(edge)], axis=0)

    far_above = lax.ppermute(end_tiles(CLON - 1, CLON - 2, several[:, -8:]), LON, forward_lon)
    far_below = lax.ppermute(end_tiles(0, 1, several[:, :8]), LON, backward_lon)

    def unpack_rows(tiles):
        edge = rows_of(tiles[2 * count + 2 * n_several :], n_single + CIN)
        return edge[:n_single], edge[n_single:]

    line_above, more_above = unpack_rows(far_above)
    line_below, more_below = unpack_rows(far_below)
    lane = jnp.arange(LANES)[None]
    valid = jnp.where(lane < CLAT, 1.0, jnp.where(lane < CLAT + LANES // 4, lat < n_lat - 1, lat > 0).astype(f32))

    def unringed(line):
        return jnp.concatenate([line[:, -1:], line[:, : CLAT + 1]], axis=1)[:, None]

    def padded(first, last):
        def ends(line):
            return unringed(line[first:last])

        middle = jnp.concatenate(
            [line_left[first:last, :, None], single[first:last], line_right[first:last, :, None]], axis=2
        )
        return jnp.concatenate([ends(line_above), middle, ends(line_below)], axis=1)

    levels = velocity.shape[0]
    feat_pad = jnp.concatenate([unringed(more_above), padded(0, CIN), unringed(more_below)], axis=1).astype(jnp.bfloat16)
    vel_pad = padded(CIN, CIN + levels)
    cot_pad = padded(CIN + levels, CIN + 2 * levels)

    gathered = to_all(merged(to_all(row, LAYER)), DEPTH).reshape(-1, 128)

    around = patches_of(feat_pad)
    hidden = jnp.tanh(jnp.dot(conv_weight, around, preferred_element_type=f32) + conv_bias[:, None])
    logits = jnp.sum(out_weight[:, None] * hidden, axis=0).reshape(CLON + 2, CLAT)
    visc_rows = jax.nn.softplus(logits)
    logits, viscosity = logits[1:-1], visc_rows[1:-1]
    columns, hidden = around[:, CLAT:-CLAT], hidden[:, CLAT:-CLAT]

    level = level_weight[:, None, None]
    first = jnp.zeros_like(viscosity)
    slopes = []
    for vel_side, cot_side in zip(neighbours(vel_pad), neighbours(cot_pad)):
        slope = vel_side - velocity
        first = first + jnp.sum(slope * (cot_side - velocity_cot), axis=0)
        slopes.append(jnp.sum(level * slope, axis=0))
    cells_all = CLON * CLAT * n_lon * n_lat
    weight = jax.nn.sigmoid(logits) * (-0.5 * time_step / math.sqrt(cells_all))

    grads, forces, sums = kernel_call(
        solve_second,
        [(3, CLON, CLAT), (2, ROWS, LANES), (1, 128)],
        gathered_first,
        gathered,
        left,
        coarse,
        right,
        above,
        below,
        far_above,
        far_below,
        several,
        valid,
        weight,
        jnp.stack(slopes),
        first,
        sums,
    )

    lines = grads.reshape(3, 1, CLON * CLAT)
    out_grad = jnp.sum(hidden[None] * lines, axis=2)
    pre = lines * (out_weight[:, None] * (1.0 - hidden * hidden))[None]
    bias_grad = jnp.sum(pre, axis=2)
    rounded = lax.reduce_precision(pre, 8, 7)
    high = rounded.astype(jnp.bfloat16)
    low = (pre - rounded).astype(jnp.bfloat16)

    def against(part):
        return lax.dot_general(
            part.reshape(3 * HID, -1), columns, (((1,), (1,)), ((), ())), preferred_element_type=f32
        )

    weight_grad = (against(high) + against(low)).reshape(3, HID, TAPS)
    each = HID // n_layer
    to = (jnp.arange(HID) // each)[:, None]
    edge = jnp.where((to == rank - 1) & (lat > 0), viscosity[None, :, 0], 0.0)
    edge = edge + jnp.where((to == rank + 1) & (lat < n_lat - 1), viscosity[None, :, -1], 0.0)
    edge = jnp.pad(edge, ((0, 0), (0, 128 - 3 * SPARE - 5 - CLON)))
    rest = jnp.concatenate([weight_grad[..., 256:], bias_grad[..., None], out_grad[..., None]], axis=2)
    table = jnp.concatenate(
        [weight_grad[k, :, :256] for k in range(3)]
        + [rest[k] for k in range(3)]
        + [jnp.broadcast_to(sums[:, :5], (HID, 5)), edge],
        axis=1,
    )
    got = exchange(table.reshape(n_layer, each, table.shape[1]), LAYER)
    part = jnp.sum(got, axis=0)
    mine, on = kernel_call(finish, [(each, 384), (1, 128)], to_all(part, DEPTH))

    to = jnp.arange(n_layer)[:, None]
    lines = got[:, 0, 6 * 128 + 3 * SPARE + 5 :][:, :CLON]
    visc_left = jnp.sum(jnp.where((to == rank - 1) & (lat > 0), lines, 0.0), axis=0)[:, None]
    visc_right = jnp.sum(jnp.where((to == rank + 1) & (lat < n_lat - 1), lines, 0.0), axis=0)[:, None]

    def rim(line):
        return jnp.pad(line, ((0, 0), (0, LANES - CLAT)))

    visc = ring_rows(ring_lanes(viscosity, visc_right, visc_left), rim(visc_rows[-1:]), rim(visc_rows[:1]))
    visc_pad = jnp.concatenate([visc[-1:], visc[: CLON + 1]], axis=0)
    visc_pad = jnp.concatenate([visc_pad[:, -1:], visc_pad[:, : CLAT + 1]], axis=1)
    (spreads,) = kernel_call(diffuse, [(2, CLON, CLAT)], visc, forces)
    base = jnp.zeros_like(velocity_cot)
    for visc_side, cot_side in zip(neighbours(visc_pad), neighbours(cot_pad)):
        base = base + 0.5 * (viscosity + visc_side)[None] * (cot_side - velocity_cot)
    base = velocity_cot + time_step * base
    final = to_all(mine, LAYER).reshape(HID, 384)
    spread = on[:, :1] * spreads[0] + on[:, 1:2] * spreads[1]
    grad_velocity = base + level * spread[None]
    return (grad_velocity, final[:, :TAPS], final[:, TAPS], final[:, TAPS + 1])


def solution(mesh):
    n_lon, n_lat = mesh.shape["lon"], mesh.shape["lat"]
    y = min(8, n_lon // 2)
    shape = (n_lon // y, y, n_lat // 2, 2)
    grid = Mesh(np.asarray(mesh.devices).reshape(shape), LON + LAT)
    tile = P(None, LON, LAT)
    flat = P(LON, LAT)
    in_specs = (tile, tile, tile, flat, flat, flat, flat, P(LON + LAT, None), P(), P(), P(), P())
    out_specs = (tile, P(), P(), P())
    return jax.shard_map(shards, mesh=grid, in_specs=in_specs, out_specs=out_specs, check_vma=False)
```

```python
import math

import jax
import jax.numpy as jnp
import numpy as np
from jax import lax
from jax.experimental import pallas as pl
from jax.experimental.pallas import tpu as pltpu
from jax.sharding import Mesh
from jax.sharding import PartitionSpec as P

CIN = 32
HID = 64
AGG = 8
CNT = 256
TAPS = 9 * CIN
time_step = 0.1

CLON = 16
CLAT = 128
HALO = 3
ROWS = 24
LANES = 256
LON = ("z", "y")
LAT = ("x", "c")
LAYER = ("y", "x", "c")
DEPTH = ("z",)
SPARE = 34


def exchange(values, axes):
    return lax.all_to_all(values, axes, 0, 0, tiled=True)


def shifted(block, axes, periodic):
    count = lax.axis_size(axes)
    forward = [(i, i + 1) for i in range(count - 1)]
    if periodic:
        forward.append((count - 1, 0))
    return forward, [(target, source) for source, target in forward]


def ring_lanes(own, right, left):
    gap = LANES - CLAT - right.shape[-1] - left.shape[-1]
    return jnp.concatenate([own, right, jnp.zeros(own.shape[:-1] + (gap,), own.dtype), left], axis=-1)


def ring_rows(own, below, above):
    gap = ROWS - CLON - below.shape[-2] - above.shape[-2]
    shape = own.shape[:-2] + (gap, own.shape[-1])
    return jnp.concatenate([own, below, jnp.zeros(shape, own.dtype), above], axis=-2)


def roll(value, shift, axis):
    return pltpu.roll(value, shift % value.shape[axis], axis)


def sides(value):
    return (roll(value, -1, 0), roll(value, 1, 0), roll(value, -1, 1), roll(value, 1, 1))


def side_sum(value):
    a, b, c, d = sides(value)
    return (a + b) + (c + d)


def coarse_column(tiles, start, vector):
    acc = tiles[start] * vector[0:1]
    for k in range(1, vector.shape[0]):
        acc = acc + tiles[start + k] * vector[k : k + 1]
    return jnp.sum(acc, axis=1, keepdims=True)


def solve_start(rhs, damp, wet, agg, columns):
    diagonal = 4.0 + damp
    z = rhs / diagonal + coarse_field(agg, *columns)
    spread = side_sum(wet * z)
    return z, diagonal * z - wet * spread, spread - 4.0 * wet * z


def ring_fields(inner, low, high):
    row = lax.broadcasted_iota(jnp.int32, (8, LANES), 0)
    return [jnp.concatenate([inner[k], jnp.where(row < 4, low[k], high[k])], axis=0) for k in range(inner.shape[0])]


def coarse_field(agg, above, middle, below):
    lane = lax.broadcasted_iota(jnp.int32, (1, CLAT), 1)
    row = lax.broadcasted_iota(jnp.int32, (ROWS - CLON, LANES), 0)

    def across(columns, k):
        left, own, right = (column[k : k + 1] for column in columns)
        side = jnp.where(lane < CLAT // 2, right, left)
        return jnp.concatenate([jnp.broadcast_to(own, (1, CLAT)), side], axis=1)

    field = jnp.zeros((ROWS, LANES), jnp.float32)
    for k in range(AGG):
        inner = jnp.broadcast_to(across(middle, k), (CLON, LANES))
        outer = jnp.where(row < (ROWS - CLON) // 2, across(below, k), across(above, k))
        field = jnp.where(agg == float(k), jnp.concatenate([inner, outer], axis=0), field)
    return field


def total(value):
    return jnp.sum(jnp.sum(value, axis=0, keepdims=True), axis=1, keepdims=True)


def restricted(value, agg, first):
    parts = [jnp.sum(jnp.where(agg == float(k), value, 0.0), axis=0, keepdims=True) for k in range(AGG)]
    sums = jnp.sum(jnp.concatenate(parts, axis=0), axis=1, keepdims=True) * (1.0 / math.sqrt(CNT))
    lane = lax.broadcasted_iota(jnp.int32, (AGG, 128), 1)
    row = lax.broadcasted_iota(jnp.int32, (AGG, 128), 0)
    return jnp.sum(jnp.where(lane == first + row, sums, 0.0), axis=0, keepdims=True)


def solve_first(place, gathered, left, coarse, right, above, below, inner, row_ref, sum_ref):
    vector = gathered[...]
    count = vector.shape[0]

    def outer(tiles):
        blank = jnp.zeros((8, LANES - CLAT), jnp.float32)
        return [jnp.concatenate([tiles[count + k], blank], axis=1) for k in range(inner.shape[0])]

    rhs, damp, wet, agg = ring_fields(inner, outer(below), outer(above))
    none = jnp.zeros((AGG, 1), jnp.float32)
    middle = [coarse_column(tiles, 0, vector) for tiles in (left, coarse, right)]
    ends = [[none, coarse_column(tiles, 0, vector), none] for tiles in (above, below)]
    z, w, force = solve_start(rhs, damp, wet, agg, (ends[0], middle, ends[1]))
    own = (slice(0, CLON), slice(0, CLAT))
    z_own, w_own = z[own], w[own]
    row_ref[...] = restricted(w_own, agg[own], place[0])
    lane = lax.broadcasted_iota(jnp.int32, (1, 128), 1)
    sum_ref[...] = jnp.where(lane == 0, total(rhs[own] * z_own), 0.0) + jnp.where(lane == 1, total(z_own * w_own), 0.0)


def solve_second(
    gathered_first, gathered, left, coarse, right, above, below, far_above, far_below, inner, valid_ref, weight_ref,
    slope_ref, first_ref, sum_in, grad_ref, force_ref, sum_ref,
):
    count = gathered.shape[0]

    def outer(tiles):
        at = 2 * count
        return [
            jnp.concatenate([tiles[at + 2 * k], tiles[at + 2 * k + 1]], axis=1) for k in range(inner.shape[0])
        ]

    def columns_of(ref):
        vector = ref[...]
        middle = [coarse_column(tiles, 0, vector) for tiles in (left, coarse, right)]
        ends = [
            [coarse_column(far, 0, vector), coarse_column(near, 0, vector), coarse_column(far, count, vector)]
            for near, far in ((above, far_above), (below, far_below))
        ]
        return ends[0], middle, ends[1]

    rhs, damp, wet, agg = ring_fields(inner, outer(far_below), outer(far_above))
    diagonal = 4.0 + damp
    z, w, leading = solve_start(rhs, damp, wet, agg, columns_of(gathered_first))
    y = w / diagonal + coarse_field(agg, *columns_of(gathered))
    around = side_sum(wet * y)
    image = diagonal * y - wet * around
    own = (slice(0, CLON), slice(0, CLAT))
    y_own = y[own]
    lane = lax.broadcasted_iota(jnp.int32, (1, 128), 1)
    sums = sum_in[...]
    for at, value in ((2, rhs[own] * y_own), (3, w[own] * y_own), (4, y_own * image[own])):
        sums = sums + jnp.where(lane == at, total(value), 0.0)
    sum_ref[...] = sums
    weight = weight_ref[...]
    grad_ref[0] = first_ref[...] * weight
    forces = (leading * valid_ref[...], (around - 4.0 * wet * y) * valid_ref[...])
    for at, force in enumerate(forces, 1):
        force_ref[at - 1] = force
        force_own = force[own]
        slope = jnp.zeros((CLON, CLAT), jnp.float32)
        for n, side in enumerate(sides(force)):
            slope = slope + slope_ref[n] * (side[own] - force_own)
        grad_ref[at] = slope * weight


def diffuse(visc_ref, forces, spread_ref):
    own = (slice(0, CLON), slice(0, CLAT))
    visc = visc_ref[...]
    visc_sides = [0.5 * (visc[own] + side[own]) for side in sides(visc)]
    for at in range(2):
        force = forces[at]
        force_own = force[own]
        bend = jnp.zeros((CLON, CLAT), jnp.float32)
        for visc_side, side in zip(visc_sides, sides(force)):
            bend = bend + visc_side * (side[own] - force_own)
        spread_ref[at] = force_own + time_step * bend


def finish(parts, mine_ref, on_ref):
    row = jnp.sum(parts[...], axis=0)
    main, tail = 2 * 128, 6 * 128

    def scalar(k):
        at = tail + 3 * SPARE + k
        return row[:1, at : at + 1]

    e0, d0, cross, ww, g = (scalar(k) for k in range(5))
    step0 = e0 / d0
    e1 = e0 - step0 * d0 - step0 * cross + step0 * step0 * ww
    beta = e1 / e0
    lead = 1.0 + beta
    pw = lead * lead * d0 - 2.0 * lead * step0 * ww + step0 * step0 * g
    step1 = e1 / pw
    on_z = step0 + step1 * lead
    on_y = -step1 * step0
    front = row[:, :main] + on_z * row[:, main : 2 * main] + on_y * row[:, 2 * main : 3 * main]
    last = row[:, tail:]
    back = last + on_z * roll(last, -SPARE, 1) + on_y * roll(last, -2 * SPARE, 1)
    mine_ref[...] = jnp.concatenate([front, back], axis=1)
    lane = lax.broadcasted_iota(jnp.int32, (1, 128), 1)
    on_ref[...] = jnp.where(lane == 0, on_z, on_y)


def neighbours(padded):
    return (padded[..., 2:, 1:-1], padded[..., :-2, 1:-1], padded[..., 1:-1, 2:], padded[..., 1:-1, :-2])


def patches_of(block):
    rows = block.shape[-2] - 2
    width = block.shape[-1] - 2
    taps = [
        block[:, first : first + rows, second : second + width]
        for first in range(3)
        for second in range(3)
    ]
    return jnp.concatenate(taps, axis=0).reshape(-1, rows * width)


def tiles_of(rows):
    count, width = rows.shape
    return rows.reshape(count // 8, 8, width // 128, 128).transpose(0, 2, 1, 3).reshape(-1, 8, 128)


def rows_of(tiles, count):
    return tiles.reshape(count // 8, -1, 8, 128).transpose(0, 2, 1, 3).reshape(count, -1)


def kernel_call(body, shapes, *args, smem=0):
    specs = [pl.BlockSpec(memory_space=pltpu.SMEM)] * smem + [pl.BlockSpec(memory_space=pltpu.VMEM)] * (len(args) - smem)
    return pl.pallas_call(
        body,
        out_shape=[jax.ShapeDtypeStruct(shape, jnp.float32) for shape in shapes],
        in_specs=specs,
        out_specs=[pl.BlockSpec(memory_space=pltpu.VMEM)] * len(shapes),
        compiler_params=pltpu.CompilerParams(vmem_limit_bytes=24 * 1024 * 1024),
    )(*args)


def shards(
    features,
    velocity,
    velocity_cot,
    surface_cot,
    damping,
    wet_mask,
    aggregate_map,
    coarse_inverse,
    conv_weight,
    conv_bias,
    out_weight,
    level_weight,
):
    f32 = jnp.float32
    n_lon, n_lat = lax.axis_size(LON), lax.axis_size(LAT)
    lon, lat = lax.axis_index(LON), lax.axis_index(LAT)
    n_layer, n_depth = lax.axis_size(LAYER), lax.axis_size(DEPTH)
    rank = lax.axis_index(LAYER)
    slot = rank % 16
    place = (slot * AGG).astype(jnp.int32)

    single = jnp.concatenate([features.astype(f32), velocity, velocity_cot], axis=0)
    inner = features.astype(f32)
    several = jnp.stack([surface_cot, damping, wet_mask.astype(f32), aggregate_map.astype(f32)])
    n_single, n_several = single.shape[0], several.shape[0]
    coarse = tiles_of(coarse_inverse)

    whole_fields = several.reshape(-1, 8, 128)

    def side_tiles(line):
        edge = jnp.pad(line, ((0, 64 - line.shape[0]), (0, 0))).reshape(1, 8, 128)
        return jnp.concatenate([coarse, whole_fields, edge], axis=0)

    forward, backward = shifted(single, LAT, False)
    left = lax.ppermute(side_tiles(single[:, :, -1]), LAT, forward)
    right = lax.ppermute(side_tiles(single[:, :, 0]), LAT, backward)

    forward_lon, backward_lon = shifted(single, LON, True)
    above = lax.ppermute(jnp.concatenate([coarse, several[:, 8:]], axis=0), LON, forward_lon)
    below = lax.ppermute(jnp.concatenate([coarse, several[:, :8]], axis=0), LON, backward_lon)

    local = restricted(surface_cot, aggregate_map.astype(f32), place)

    def merged(got):
        lane_slot = jnp.arange(128)[None, None] // AGG
        kept = jnp.where(lane_slot == jnp.arange(16)[None, :, None], got.reshape(-1, 16, 128), 0.0)
        return jnp.sum(kept, axis=1)

    def to_all(block, axes):
        return exchange(jnp.broadcast_to(block[None], (lax.axis_size(axes),) + block.shape), axes)

    row = merged(to_all(local, LAYER))
    gathered_first = to_all(row, DEPTH).reshape(-1, 128)
    unused, left, right = lax.optimization_barrier((row, left, right))

    count = coarse.shape[0]
    line_left = left[-1].reshape(64, CLON)[:n_single]
    line_right = right[-1].reshape(64, CLON)[:n_single]
    lane = jnp.arange(CLAT)[None, None]
    rest = jnp.where(lane < CLAT // 2, right[count:-1].reshape(several.shape), left[count:-1].reshape(several.shape))
    several = jnp.concatenate([several, rest], axis=2)
    row, sums = kernel_call(
        solve_first,
        [(1, 128), (1, 128)],
        place[None],
        gathered_first,
        left,
        coarse,
        right,
        above,
        below,
        several,
        smem=1,
    )
    band = jnp.concatenate([left[:count], right[:count]], axis=0)

    def end_tiles(at, second, block):
        line = ring_lanes(single[:, at, :], line_right[:, at : at + 1], line_left[:, at : at + 1])
        more = ring_lanes(
            inner[:, second, :], line_right[:CIN, second : second + 1], line_left[:CIN, second : second + 1]
        )
        edge = jnp.concatenate([block.reshape(-1, LANES), line, more], axis=0)
        return jnp.concatenate([band, tiles_of(edge)], axis=0)

    far_above = lax.ppermute(end_tiles(CLON - 1, CLON - 2, several[:, -8:]), LON, forward_lon)
    far_below = lax.ppermute(end_tiles(0, 1, several[:, :8]), LON, backward_lon)

    def unpack_rows(tiles):
        edge = rows_of(tiles[2 * count + 2 * n_several :], n_single + CIN)
        return edge[:n_single], edge[n_single:]

    line_above, more_above = unpack_rows(far_above)
    line_below, more_below = unpack_rows(far_below)
    lane = jnp.arange(LANES)[None]
    valid = jnp.where(lane < CLAT, 1.0, jnp.where(lane < CLAT + LANES // 4, lat < n_lat - 1, lat > 0).astype(f32))

    def unringed(line):
        return jnp.concatenate([line[:, -1:], line[:, : CLAT + 1]], axis=1)[:, None]

    def padded(first, last):
        def ends(line):
            return unringed(line[first:last])

        middle = jnp.concatenate(
            [line_left[first:last, :, None], single[first:last], line_right[first:last, :, None]], axis=2
        )
        return jnp.concatenate([ends(line_above), middle, ends(line_below)], axis=1)

    levels = velocity.shape[0]
    feat_pad = jnp.concatenate([unringed(more_above), padded(0, CIN), unringed(more_below)], axis=1).astype(jnp.bfloat16)
    vel_pad = padded(CIN, CIN + levels)
    cot_pad = padded(CIN + levels, CIN + 2 * levels)

    gathered = to_all(merged(to_all(row, LAYER)), DEPTH).reshape(-1, 128)

    around = patches_of(feat_pad)
    hidden = jnp.tanh(jnp.dot(conv_weight, around, preferred_element_type=f32) + conv_bias[:, None])
    logits = jnp.sum(out_weight[:, None] * hidden, axis=0).reshape(CLON + 2, CLAT)
    visc_rows = jax.nn.softplus(logits)
    logits, viscosity = logits[1:-1], visc_rows[1:-1]
    columns, hidden = around[:, CLAT:-CLAT], hidden[:, CLAT:-CLAT]

    level = level_weight[:, None, None]
    first = jnp.zeros_like(viscosity)
    slopes = []
    for vel_side, cot_side in zip(neighbours(vel_pad), neighbours(cot_pad)):
        slope = vel_side - velocity
        first = first + jnp.sum(slope * (cot_side - velocity_cot), axis=0)
        slopes.append(jnp.sum(level * slope, axis=0))
    cells_all = CLON * CLAT * n_lon * n_lat
    weight = jax.nn.sigmoid(logits) * (-0.5 * time_step / math.sqrt(cells_all))

    grads, forces, sums = kernel_call(
        solve_second,
        [(3, CLON, CLAT), (2, ROWS, LANES), (1, 128)],
        gathered_first,
        gathered,
        left,
        coarse,
        right,
        above,
        below,
        far_above,
        far_below,
        several,
        valid,
        weight,
        jnp.stack(slopes),
        first,
        sums,
    )

    lines = grads.reshape(3, 1, CLON * CLAT)
    out_grad = jnp.sum(hidden[None] * lines, axis=2)
    pre = lines * (out_weight[:, None] * (1.0 - hidden * hidden))[None]
    bias_grad = jnp.sum(pre, axis=2)
    rounded = lax.reduce_precision(pre, 8, 7)
    high = rounded.astype(jnp.bfloat16)
    low = (pre - rounded).astype(jnp.bfloat16)

    def against(part):
        return lax.dot_general(
            part.reshape(3 * HID, -1), columns, (((1,), (1,)), ((), ())), preferred_element_type=f32
        )

    weight_grad = (against(high) + against(low)).reshape(3, HID, TAPS)
    each = HID // n_layer
    to = (jnp.arange(HID) // each)[:, None]
    edge = jnp.where((to == rank - 1) & (lat > 0), viscosity[None, :, 0], 0.0)
    edge = edge + jnp.where((to == rank + 1) & (lat < n_lat - 1), viscosity[None, :, -1], 0.0)
    edge = jnp.pad(edge, ((0, 0), (0, 128 - 3 * SPARE - 5 - CLON)))
    rest = jnp.concatenate([weight_grad[..., 256:], bias_grad[..., None], out_grad[..., None]], axis=2)
    table = jnp.concatenate(
        [weight_grad[k, :, :256] for k in range(3)]
        + [rest[k] for k in range(3)]
        + [jnp.broadcast_to(sums[:, :5], (HID, 5)), edge],
        axis=1,
    )
    got = exchange(table.reshape(n_layer, each, table.shape[1]), LAYER)
    part = jnp.sum(got, axis=0)
    mine, on = kernel_call(finish, [(each, 384), (1, 128)], to_all(part, DEPTH))

    to = jnp.arange(n_layer)[:, None]
    lines = got[:, 0, 6 * 128 + 3 * SPARE + 5 :][:, :CLON]
    visc_left = jnp.sum(jnp.where((to == rank - 1) & (lat > 0), lines, 0.0), axis=0)[:, None]
    visc_right = jnp.sum(jnp.where((to == rank + 1) & (lat < n_lat - 1), lines, 0.0), axis=0)[:, None]

    def rim(line):
        return jnp.pad(line, ((0, 0), (0, LANES - CLAT)))

    visc = ring_rows(ring_lanes(viscosity, visc_right, visc_left), rim(visc_rows[-1:]), rim(visc_rows[:1]))
    visc_pad = jnp.concatenate([visc[-1:], visc[: CLON + 1]], axis=0)
    visc_pad = jnp.concatenate([visc_pad[:, -1:], visc_pad[:, : CLAT + 1]], axis=1)
    (spreads,) = kernel_call(diffuse, [(2, CLON, CLAT)], visc, forces)
    base = jnp.zeros_like(velocity_cot)
    for visc_side, cot_side in zip(neighbours(visc_pad), neighbours(cot_pad)):
        base = base + 0.5 * (viscosity + visc_side)[None] * (cot_side - velocity_cot)
    base = velocity_cot + time_step * base
    final = to_all(mine, LAYER).reshape(HID, 384)
    spread = on[:, :1] * spreads[0] + on[:, 1:2] * spreads[1]
    grad_velocity = base + level * spread[None]
    return (grad_velocity, final[:, :TAPS], final[:, TAPS], final[:, TAPS + 1])


def solution(mesh):
    n_lon, n_lat = mesh.shape["lon"], mesh.shape["lat"]
    y = min(8, n_lon // 2)
    shape = (n_lon // y, y, n_lat // 2, 2)
    grid = Mesh(np.asarray(mesh.devices).reshape(shape), LON + LAT)
    tile = P(None, LON, LAT)
    flat = P(LON, LAT)
    in_specs = (tile, tile, tile, flat, flat, flat, flat, P(LON + LAT, None), P(), P(), P(), P())
    out_specs = (tile, P(), P(), P())
    return jax.shard_map(shards, mesh=grid, in_specs=in_specs, out_specs=out_specs, check_vma=False)
```
